32 devices in a mesh: parts: 2 (over y), shard: 4 (over z), grp: 2 (over x), sub: 2 (over core).
Axes of the slice: x: 2, y: 2, z: 4, core: 2. Of those that a mesh axis runs over, the one named last changes fastest.
Arguments:
- embeddings: float32 [16384, 1024], P(('parts', 'shard', 'grp', 'sub')), parts along dimension 0, may hold values from -120 to 120
- labels: int32 [16384], P(('parts', 'shard', 'grp', 'sub')), parts along dimension 0, may hold values from 0 to 4095, as said below
- doc_block: int32 [16384], P(('parts', 'shard', 'grp', 'sub')), parts along dimension 0, may hold values from 0 to 3
- assign: int32 [8192], P('parts'), parts along dimension 0, may hold values from 0 to 3, as said below
- pattern: int32 [4, 4], replicated, may hold values 0 or 1
Outputs:
- doc_max: float32 [16384], P(('parts', 'shard', 'grp', 'sub')), parts along dimension 0
The draws below stay inside these ranges and needn't reach their ends.
There are 2 independent parts, one for each index of `parts`. The reference program is written for one: setup_inputs(seed, part) draws one part's arguments, and reference() takes and returns one part's arrays. A program takes and returns all parts, laid end to end along the dimension named above; an argument that names none is the same for every part. Nothing has to cross between parts.
Inputs may be any that keep to these rules, and one draw needn't show every extreme that they name: `labels`: in each aligned block of 512 documents (the documents of one device) at most 256 have a cluster that assign maps to any one group; one group, the same for every block of a part, gets exactly 256 from every block. Split the clusters of a group, starting at cluster s with e clusters, into 4 ranges, range k holding clusters s + (k * e) // 4 up to the start of range k + 1; of the documents that one block sends to one group at most 64 fall into any one range, and the group that gets 256 from every block gets exactly that many in every range. `assign`: Non-decreasing over the clusters; every group owns at least 8 clusters.
All inputs are finite; a program needn't handle non-finite values.
Results may differ from the reference program's by a relative error of at most 0.0003.
Values may be sent and summed in bfloat16 or wider, within the bound.
No kernel may reach another device: no remote copies, remote signals or barrier semaphores. Data moves between devices by JAX's collectives and lax.ppermute only.
A program may use at most 64 MiB of HBM per device.

```python
import jax
import jax.numpy as jnp
from jax import lax

D = 1024
CLUSTERS = 4096
NBLK = 4
DOC_DEV = 512
CAP = 256
DOCS = 8192
N_SHARD = 4
N_GRP = 2
N_SUB = 2


def layout(base):
    subkeys = jax.random.split(base, 6)
    members_total = N_GRP * N_SUB
    least_extent = 2 * members_total
    spare = CLUSTERS - N_SHARD * least_extent
    cut_points = jnp.sort(jax.random.randint(subkeys[0], (N_SHARD - 1,), 0, spare + 1)).astype(jnp.int32)
    boundaries = (jnp.arange(1, N_SHARD, dtype=jnp.int32) * least_extent + cut_points).astype(jnp.int32)
    cluster_ids = jnp.arange(CLUSTERS, dtype=jnp.int32)
    assign = jnp.sum((cluster_ids[:, None] >= boundaries[None, :]).astype(jnp.int32), axis=1)
    starts = jnp.concatenate([jnp.zeros((1,), jnp.int32), boundaries])
    extent = jnp.concatenate([boundaries, jnp.full((1,), CLUSTERS, jnp.int32)]) - starts
    devices = DOCS // DOC_DEV
    slot_total = N_SHARD * CAP
    slot_group = jnp.arange(slot_total, dtype=jnp.int32) // CAP
    favored = jax.random.randint(subkeys[1], (), 0, N_SHARD)
    weight = jax.random.randint(subkeys[2], (N_SHARD,), 0, 4)
    jitter = jax.random.randint(subkeys[3], (devices, N_SHARD), 0, 2)
    preference = weight[None, :] + jitter
    preference = jnp.where(jnp.arange(N_SHARD, dtype=jnp.int32)[None, :] == favored, 8, preference)
    tiebreak = jax.random.randint(subkeys[4], (devices, slot_total), 0, 4096)
    slot_score = (preference[:, slot_group] * 4096 + tiebreak) * slot_total + jnp.arange(slot_total, dtype=jnp.int32)[None, :]
    chosen = lax.top_k(slot_score, DOC_DEV)[1]
    destination = (chosen // CAP).astype(jnp.int32)
    shuffle_score = jax.random.randint(subkeys[5], (devices, DOC_DEV), 0, 1 << 20) * DOC_DEV + jnp.arange(DOC_DEV, dtype=jnp.int32)[None, :]
    shuffle_order = jnp.argsort(shuffle_score, axis=1)
    destination = jnp.take_along_axis(destination, shuffle_order, axis=1)
    dest_hot = (destination[:, :, None] == jnp.arange(N_SHARD, dtype=jnp.int32)[None, None, :]).astype(jnp.int32)
    ahead = jnp.cumsum(dest_hot, axis=1) - dest_hot
    rank = jnp.sum(ahead * dest_hot, axis=2)
    range_id = rank % members_total
    range_low = starts[destination] + range_id * extent[destination] // members_total
    range_high = starts[destination] + (range_id + 1) * extent[destination] // members_total
    within_pick = jax.random.randint(jax.random.fold_in(subkeys[5], 1), (devices, DOC_DEV), 0, 1 << 20)
    labels = range_low + within_pick % (range_high - range_low)
    return (assign, labels.reshape(DOCS).astype(jnp.int32))


def draw_labels(key, part):
    return layout(key)[1]


def draw_assign(key, part):
    return layout(key)[0]


def draw_embeddings(key, part):
    labels = layout(key)[1]
    key = jax.random.fold_in(key, 11)
    key_bit, key_shared, key_noise = jax.random.split(key, 3)
    shared_bit = jax.random.randint(key_bit, (DOCS,), 0, 2)

    def vector(index):
        return jax.random.normal(jax.random.fold_in(key_shared, index), (D,), jnp.float32)
    shared_vec = jax.vmap(vector)(labels + shared_bit)
    noise_part = 0.5 * jax.random.normal(key_noise, (DOCS, D), jnp.float32)
    return jnp.clip(shared_vec + noise_part, -120.0, 120.0)


def with_ends(array, key, low, high):
    place = [jax.random.randint(jax.random.fold_in(key, axis), (), 0, length) for axis, length in enumerate(array.shape)]
    main_axis = array.shape.index(max(array.shape))
    beside = place[:main_axis] + [(place[main_axis] + 1) % array.shape[main_axis]] + place[main_axis + 1:]
    return array.at[tuple(place)].set(low).at[tuple(beside)].set(high)


def setup_inputs(seed: int = 0, part: int = 0) -> dict:
    keys = jax.random.split(jax.random.key(seed), 6)
    own_keys = jax.random.split(jax.random.fold_in(keys[5], part), 6)
    embeddings = draw_embeddings(jax.random.fold_in(jax.random.fold_in(keys[5], part), 71), part)
    labels = draw_labels(jax.random.fold_in(jax.random.fold_in(keys[5], part), 71), part)
    doc_block = with_ends(jax.random.randint(own_keys[2], (DOCS,), 0, NBLK), jax.random.fold_in(own_keys[2], 1), 0, NBLK - 1).astype(jnp.int32)
    assign = draw_assign(jax.random.fold_in(jax.random.fold_in(keys[5], part), 71), part)
    pattern = with_ends((jax.random.randint(keys[4], (NBLK, NBLK), 0, 4) < 3).astype(jnp.int32), jax.random.fold_in(keys[4], 1), 0, 1)
    return dict(embeddings=embeddings, labels=labels, doc_block=doc_block, assign=assign, pattern=pattern)


def row_masks(doc_codes, pattern):
    count = pattern.shape[0]
    powers = jnp.left_shift(jnp.int32(1), jnp.arange(count, dtype=jnp.int32))
    pattern_bits = lax.optimization_barrier(jnp.sum(pattern * powers[None, :], axis=1))
    block_ids = doc_codes % count
    picked = block_ids[:, None] == jnp.arange(count, dtype=jnp.int32)[None, :]
    return lax.optimization_barrier(jnp.sum(jnp.where(picked, pattern_bits[None, :], 0), axis=1))

def allowed(row_codes, masks, col_codes, count):
    adjacent = jnp.abs(row_codes[:, None] // count - col_codes[None, :] // count) <= 1
    filled = (col_codes >= 0)[None, :]
    permitted = jnp.right_shift(masks[:, None], col_codes[None, :] % count) % 2 == 1
    return adjacent & filled & permitted

def reference(embeddings, labels, doc_block, assign, pattern):
    count = pattern.shape[0]
    unit_rows = (embeddings * lax.rsqrt(lax.optimization_barrier(jnp.sum(embeddings * embeddings, axis=1, keepdims=True)) + 1e-06)).astype(jnp.bfloat16)
    target_group = assign[labels].astype(jnp.int32)
    doc_codes = (labels * count + doc_block).astype(jnp.int32)
    sort_order = jnp.argsort(target_group, stable=True).astype(jnp.int32)
    counts = lax.optimization_barrier(jnp.sum((target_group[:, None] == jnp.arange(N_SHARD, dtype=jnp.int32)[None, :]).astype(jnp.int32), axis=0))
    starts = (jnp.cumsum(counts) - counts).astype(jnp.int32)
    group_rows = 2 * DOC_DEV * N_GRP * N_SUB
    sorted_unit = jnp.concatenate([unit_rows[sort_order], jnp.zeros((group_rows, D), jnp.bfloat16)])
    sorted_codes = jnp.concatenate([doc_codes[sort_order], jnp.full((group_rows,), -1, jnp.int32)])

    def per_group(group_id):
        opening = starts[group_id]
        members_unit = lax.dynamic_slice_in_dim(sorted_unit, opening, group_rows, 0)
        member_codes = lax.dynamic_slice_in_dim(sorted_codes, opening, group_rows, 0)
        inside = jnp.arange(group_rows, dtype=jnp.int32) < counts[group_id]
        member_codes = jnp.where(inside, member_codes, -1)
        similarity = jnp.dot(members_unit, members_unit.T, preferred_element_type=jnp.float32)
        permitted_pairs = allowed(member_codes, row_masks(member_codes, pattern), member_codes, count)
        permitted_pairs = permitted_pairs & ~jnp.eye(group_rows, dtype=bool)
        return lax.optimization_barrier(jnp.max(jnp.where(permitted_pairs, similarity, -1.0), axis=1))
    results = lax.map(per_group, jnp.arange(N_SHARD, dtype=jnp.int32))
    sorted_rank = jnp.zeros((DOCS,), jnp.int32).at[sort_order].set(jnp.arange(DOCS, dtype=jnp.int32))
    return results[target_group, sorted_rank - starts[target_group]]
```

```python
import functools
import math

import jax
import jax.numpy as jnp
from jax import lax
from jax.experimental import pallas as pl
from jax.experimental.pallas import tpu as pltpu
from jax.sharding import PartitionSpec as P

BF16 = jnp.bfloat16
F32 = jnp.float32
VMEM_LIMIT = 48 * 1024 * 1024
LANES = 128
BARRED = 4.0


def row_masks(doc_codes, pattern):
    count = pattern.shape[0]
    powers = jnp.left_shift(jnp.int32(1), jnp.arange(count, dtype=jnp.int32))
    pattern_bits = jnp.sum(pattern * powers[None, :], axis=1)
    block_ids = doc_codes % count
    picked = block_ids[:, None] == jnp.arange(count, dtype=jnp.int32)[None, :]
    return jnp.sum(jnp.where(picked, pattern_bits[None, :], 0), axis=1)


def allowed(row_codes, masks, col_codes, count):
    adjacent = jnp.abs(row_codes[:, None] // count - col_codes[None, :] // count) <= 1
    filled = (col_codes >= 0)[None, :]
    permitted = jnp.right_shift(masks[:, None], col_codes[None, :] % count) % 2 == 1
    return adjacent & filled & permitted


def scores(left_rows, right_rows):
    return lax.dot_general(
        left_rows, right_rows, (((1,), (1,)), ((), ())), preferred_element_type=jnp.float32
    )


def from_members(rows):
    members = lax.axis_size(("grp", "sub"))
    shifts = [[(i, (i + shift) % members) for i in range(members)] for shift in range(1, members)]
    return jnp.concatenate([rows] + [lax.ppermute(rows, ("grp", "sub"), to) for to in shifts])


def general_form(embeddings, labels, doc_block, assign, pattern):
    count = pattern.shape[0]
    group_count = lax.axis_size("shard")
    local_rows = embeddings.shape[0]
    capacity = 2 * local_rows // group_count
    features = embeddings.shape[1]
    unit_rows = (
        embeddings * lax.rsqrt(jnp.sum(embeddings * embeddings, axis=1, keepdims=True) + 1e-06)
    ).astype(jnp.bfloat16)
    target_group = assign[labels]
    one_hot = (target_group[:, None] == jnp.arange(group_count, dtype=jnp.int32)[None, :]).astype(
        jnp.int32
    )
    earlier = jnp.cumsum(one_hot, axis=0) - one_hot
    send_slot = target_group * capacity + jnp.sum(earlier * one_hot, axis=1)
    doc_codes = labels * count + doc_block
    outgoing = (
        jnp.zeros((group_count * capacity, features), jnp.bfloat16).at[send_slot].set(unit_rows)
    )
    outgoing_codes = jnp.full((group_count * capacity,), -1, jnp.int32).at[send_slot].set(doc_codes)
    arrived, arrived_codes = (
        lax.all_to_all(outgoing, "shard", split_axis=0, concat_axis=0, tiled=True),
        lax.all_to_all(outgoing_codes, "shard", split_axis=0, concat_axis=0, tiled=True),
    )
    masks = row_masks(arrived_codes, pattern)
    row_count = arrived.shape[0]
    position = jnp.arange(row_count, dtype=jnp.int32)
    start_value = jnp.full((row_count,), -1.0, jnp.float32)
    columns = from_members(arrived)
    column_codes = from_members(arrived_codes)
    similarity = scores(arrived, columns)
    permitted_pairs = allowed(arrived_codes, masks, column_codes, count)
    column_position = jnp.arange(columns.shape[0], dtype=jnp.int32)
    permitted_pairs = permitted_pairs & (position[:, None] != column_position[None, :])
    best_match = jnp.maximum(
        start_value, jnp.max(jnp.where(permitted_pairs, similarity, -1.0), axis=1)
    )
    returned_max = lax.all_to_all(best_match, "shard", split_axis=0, concat_axis=0, tiled=True)
    return returned_max[send_slot]


def dot_nt(left, right):
    return lax.dot_general(left, right, (((1,), (1,)), ((), ())), preferred_element_type=F32)


def pack_kernel(
    groups, chips, cores, slots, count, emb_ref, label_ref, block_ref, assign_ref, out_ref, slot_ref
):
    docs, features = emb_ref.shape
    part = features // cores
    labels = label_ref[...]
    clusters = assign_ref.shape[0] * assign_ref.shape[1]
    assign = assign_ref[...]

    group = jnp.zeros((1, docs), jnp.int32)
    start = jnp.zeros((1, docs), jnp.int32)
    stop = jnp.full((1, docs), clusters, jnp.int32)
    for g in range(1, groups):
        bound = jnp.sum((assign < g).astype(F32), axis=0, keepdims=True)
        bound = jnp.sum(bound, axis=1, keepdims=True).astype(jnp.int32)
        inside = labels >= bound
        group = group + inside.astype(jnp.int32)
        start = jnp.where(inside, jnp.maximum(start, bound), start)
        stop = jnp.where(inside, stop, jnp.minimum(stop, bound))
    extent = (stop - start).astype(F32)

    def home_of(cluster):
        above = ((cluster - start + 1) * chips - 1).astype(F32)
        return jnp.floor((above + 0.5) / extent).astype(jnp.int32)

    home = home_of(labels)
    beside = jnp.where(labels + 1 < stop, home_of(labels + 1), home)

    chip_id = lax.broadcasted_iota(jnp.int32, (chips, docs), 0)
    member = (chip_id == home) | (chip_id == beside)
    earlier = (
        lax.broadcasted_iota(jnp.int32, (docs, docs), 0)
        < lax.broadcasted_iota(jnp.int32, (docs, docs), 1)
    ).astype(F32).astype(BF16)
    rank = jnp.dot(
        member.astype(F32).astype(BF16), earlier, preferred_element_type=F32
    ).astype(jnp.int32)
    over = jnp.max((member & (rank >= slots - 1)).astype(F32), axis=0, keepdims=True)
    over = jnp.max(over, axis=1, keepdims=True)
    slot = jnp.where(member & (rank < slots - 1), rank, -1)
    slot_ref[...] = slot

    code = (labels + group) * count + block_ref[...] + 1
    row_id = lax.broadcasted_iota(jnp.int32, (8, docs), 0)
    digits = jnp.where(row_id == 0, code >> 7, jnp.where(row_id == 1, code & 127, 0))
    digits = digits.astype(F32).astype(BF16)

    slot_id = lax.broadcasted_iota(jnp.int32, (chips, slots, docs), 1)
    picks = (slot_id == slot[:, None, :]).astype(F32).reshape(chips * slots, docs).astype(BF16)

    lane_slot = lax.broadcasted_iota(jnp.int32, (LANES, docs), 0)
    code_rows = []
    for chip in range(chips):
        pick = (lane_slot == slot[chip : chip + 1, :]).astype(F32).astype(BF16)
        sent = dot_nt(digits, pick)
        row = [sent[0:1, :], sent[1:2, :], jnp.broadcast_to(over, (1, LANES))]
        row.append(jnp.zeros((1, part - 3 * LANES), F32))
        code_rows.append(jnp.concatenate(row, axis=1))
    code_rows = jnp.concatenate(code_rows, axis=0)

    emb = emb_ref[...]
    unit = (emb * lax.rsqrt(jnp.sum(emb * emb, axis=1, keepdims=True) + 1e-06)).astype(BF16)
    last = lax.broadcasted_iota(jnp.int32, (chips, slots, part), 1) == slots - 1
    for core in range(cores):
        rows = jnp.dot(
            picks, unit[:, core * part : (core + 1) * part], preferred_element_type=F32
        ).reshape(chips, slots, part)
        rows = jnp.where(last, code_rows[:, None, :], rows).reshape(chips * slots, part)
        out_ref[core * chips * slots : (core + 1) * chips * slots, :] = rows.astype(BF16)


def match_kernel(
    chips, cores, slots, core_ref, own_ref, other_ref, pattern_ref, best_ref, code_ref
):
    half = chips * slots
    total = cores * half
    core = core_ref[0]
    sources = cores * chips

    at_row = lax.broadcasted_iota(jnp.int32, (sources, total), 1)
    source = lax.broadcasted_iota(jnp.int32, (sources, total), 0)
    pick = (at_row == source * slots + slots - 1).astype(F32).astype(BF16)
    sent = jnp.dot(pick, own_ref[:, : 2 * LANES], preferred_element_type=F32)
    lane_of = lax.broadcasted_iota(jnp.int32, (LANES, total), 0)
    col_of = lax.broadcasted_iota(jnp.int32, (LANES, total), 1)
    spread = (lane_of == lax.rem(col_of, slots)).astype(F32).astype(BF16)
    mine = lax.div(at_row, slots) == source
    high = jnp.dot(sent[:, :LANES].astype(BF16), spread, preferred_element_type=F32)
    low = jnp.dot(sent[:, LANES : 2 * LANES].astype(BF16), spread, preferred_element_type=F32)
    code = jnp.sum(jnp.where(mine, high * 128.0 + low, 0.0), axis=0, keepdims=True) - 1.0
    count = pattern_ref.shape[0]
    label = jnp.floor((code + 0.5) / count)
    label = jnp.where(code < 0.0, -8.0, label)
    block = jnp.where(code < 0.0, -1.0, code - label * count)

    code_ref[:, 0:1] = jnp.transpose(jnp.broadcast_to(label, (8, total)))[:, 0:1]
    code_ref[:, 1:2] = jnp.transpose(jnp.broadcast_to(block, (8, total)))[:, 0:1]

    lane = lax.broadcasted_iota(jnp.int32, (half, LANES), 1).astype(F32)
    wide = jnp.zeros((LANES, LANES), F32)
    from_block = lax.broadcasted_iota(jnp.int32, (LANES, LANES), 0)
    to_block = lax.broadcasted_iota(jnp.int32, (LANES, LANES), 1)
    for a in range(count):
        for b in range(count):
            term = BARRED * (pattern_ref[a, b].astype(F32) - 1.0)
            wide = jnp.where((from_block == a) & (to_block == b), term, wide)
    base = pl.multiple_of(core * half, 16)
    row_label = code_ref[pl.ds(base, half), 0:1]
    row_hot = (lane == code_ref[pl.ds(base, half), 1:2]).astype(F32).astype(BF16)
    row_terms = jnp.dot(row_hot, wide.astype(BF16), preferred_element_type=F32).astype(BF16)
    row_label = jnp.broadcast_to(row_label, (half, LANES))
    left_own = own_ref[pl.ds(base, half), :]
    left_other = other_ref[pl.ds(base, half), :]

    best = jnp.full((half, LANES), -1.0, F32)
    row_at = lax.broadcasted_iota(jnp.int32, (half, LANES), 0)
    col_at = lax.broadcasted_iota(jnp.int32, (half, LANES), 1)
    step = 2 * LANES
    label_cols = jnp.broadcast_to(label, (8, total))
    for turn in range(cores):
        which = lax.rem(core + turn, cores)
        begin = pl.multiple_of(which * half, 16)
        labels_here = label_cols[:, 0:half]
        for k in range(1, cores):
            labels_here = jnp.where(which == k, label_cols[:, k * half : (k + 1) * half], labels_here)
        for at in range(0, half, step):
            width = min(step, half - at)
            offset = pl.multiple_of(begin + at, 16)
            sim = dot_nt(left_own, own_ref[pl.ds(offset, width), :])
            sim += dot_nt(left_other, other_ref[pl.ds(offset, width), :])
            lane_w = lax.broadcasted_iota(jnp.int32, (width, LANES), 1).astype(F32)
            hot = (lane_w == code_ref[pl.ds(offset, width), 1:2]).astype(F32).astype(BF16)
            sim += dot_nt(row_terms, hot)
            for piece in range(0, width, LANES):
                span = min(LANES, width - piece)
                gap = row_label[:, :span] - labels_here[0:1, at + piece : at + piece + span]
                near = jnp.abs(gap) <= 1.0
                if turn == 0:
                    near = near & (row_at[:, :span] != col_at[:, :span] + (at + piece))
                value = jnp.where(near, sim[:, piece : piece + span], -1.0)
                if span < LANES:
                    value = jnp.concatenate(
                        [value, jnp.full((half, LANES - span), -1.0, F32)], axis=1
                    )
                best = jnp.maximum(best, value)
    across = jnp.max(jnp.transpose(best), axis=0, keepdims=True)
    for chip in range(chips):
        best_ref[chip : chip + 1, 0:slots] = across[:, chip * slots : (chip + 1) * slots]


def unpack_kernel(chips, slots, back_ref, slot_ref, out_ref):
    docs = slot_ref.shape[1]
    back = jnp.transpose(back_ref[...])
    slot_id = lax.broadcasted_iota(jnp.int32, (slots, docs), 0)
    best = jnp.full((slots, docs), -1.0, F32)
    for chip in range(chips):
        here = slot_id == slot_ref[chip : chip + 1, :]
        best = jnp.maximum(best, jnp.where(here, back[0:slots, chip : chip + 1], -1.0))
    out_ref[...] = jnp.max(best, axis=0, keepdims=True)


def in_vmem():
    return pl.BlockSpec(memory_space=pltpu.VMEM)


def in_smem():
    return pl.BlockSpec(memory_space=pltpu.SMEM)


def per_device(embeddings, labels, doc_block, assign, pattern):
    groups = lax.axis_size("shard")
    chips = groups * lax.axis_size("grp")
    cores = lax.axis_size("sub")
    docs, features = embeddings.shape
    count = pattern.shape[0]
    mean = docs // chips
    slots = -(-(mean + int(3 * math.sqrt(mean))) // 8) * 8
    half = chips * slots
    part = features // cores
    params = pltpu.CompilerParams(vmem_limit_bytes=VMEM_LIMIT)

    outgoing, slot = pl.pallas_call(
        functools.partial(pack_kernel, groups, chips, cores, slots, count),
        out_shape=(
            jax.ShapeDtypeStruct((cores * half, part), BF16),
            jax.ShapeDtypeStruct((chips, docs), jnp.int32),
        ),
        in_specs=[in_vmem()] * 4,
        out_specs=(in_vmem(), in_vmem()),
        compiler_params=params,
        name="pack",
    )(
        embeddings,
        labels.reshape(1, docs),
        doc_block.reshape(1, docs),
        assign.reshape(-1, LANES),
    )
    arrived = lax.all_to_all(
        outgoing, ("sub", "shard", "grp"), split_axis=0, concat_axis=0, tiled=True
    )
    swapped = lax.ppermute(arrived, "sub", [(i, (i + 1) % cores) for i in range(cores)])
    core = lax.axis_index("sub").astype(jnp.int32).reshape(1)
    over = arrived.reshape(cores * chips, slots, part)[:, slots - 1, 2 * LANES : 3 * LANES]
    over = jnp.max(over.astype(F32), axis=0, keepdims=True)
    parts = lax.axis_size("parts")
    for shift in range(1, parts):
        to = [(i, (i + shift) % parts) for i in range(parts)]
        over = jnp.maximum(over, lax.ppermute(over, "parts", to))
    best = pl.pallas_call(
        functools.partial(match_kernel, chips, cores, slots),
        out_shape=jax.ShapeDtypeStruct((chips, LANES), F32),
        in_specs=[in_smem(), in_vmem(), in_vmem(), in_smem()],
        out_specs=in_vmem(),
        scratch_shapes=[pltpu.VMEM((cores * half, LANES), F32)],
        compiler_params=params,
        name="match",
    )(core, arrived, swapped, pattern)
    back = lax.all_to_all(best, ("shard", "grp"), split_axis=0, concat_axis=0, tiled=True)
    found = pl.pallas_call(
        functools.partial(unpack_kernel, chips, slots),
        out_shape=jax.ShapeDtypeStruct((1, docs), F32),
        in_specs=[in_vmem()] * 2,
        out_specs=in_vmem(),
        compiler_params=params,
        name="unpack",
    )(back, slot).reshape(docs)
    return lax.cond(
        over[0, 0] > 0.0,
        lambda: general_form(embeddings, labels, doc_block, assign, pattern),
        lambda: found,
    )


def solution(mesh):
    in_specs = (
        P(("parts", "shard", "grp", "sub"), None),
        P(("parts", "shard", "grp", "sub")),
        P(("parts", "shard", "grp", "sub")),
        P("parts"),
        P(),
    )
    out_specs = P(("parts", "shard", "grp", "sub"))
    return jax.shard_map(
        per_device, mesh=mesh, in_specs=in_specs, out_specs=out_specs, check_vma=False
    )
```

```python
import functools
import math

import jax
import jax.numpy as jnp
from jax import lax
from jax.experimental import pallas as pl
from jax.experimental.pallas import tpu as pltpu
from jax.sharding import PartitionSpec as P

BF16 = jnp.bfloat16
F32 = jnp.float32
VMEM_LIMIT = 48 * 1024 * 1024
LANES = 128
MORE = 40
BARRED = 4.0


def row_masks(doc_codes, pattern):
    count = pattern.shape[0]
    powers = jnp.left_shift(jnp.int32(1), jnp.arange(count, dtype=jnp.int32))
    pattern_bits = jnp.sum(pattern * powers[None, :], axis=1)
    block_ids = doc_codes % count
    picked = block_ids[:, None] == jnp.arange(count, dtype=jnp.int32)[None, :]
    return jnp.sum(jnp.where(picked, pattern_bits[None, :], 0), axis=1)


def allowed(row_codes, masks, col_codes, count):
    adjacent = jnp.abs(row_codes[:, None] // count - col_codes[None, :] // count) <= 1
    filled = (col_codes >= 0)[None, :]
    permitted = jnp.right_shift(masks[:, None], col_codes[None, :] % count) % 2 == 1
    return adjacent & filled & permitted


def scores(left_rows, right_rows):
    return lax.dot_general(
        left_rows, right_rows, (((1,), (1,)), ((), ())), preferred_element_type=jnp.float32
    )


def from_members(rows):
    members = lax.axis_size(("grp", "sub"))
    shifts = [[(i, (i + shift) % members) for i in range(members)] for shift in range(1, members)]
    return jnp.concatenate([rows] + [lax.ppermute(rows, ("grp", "sub"), to) for to in shifts])


def general_form(embeddings, labels, doc_block, assign, pattern):
    count = pattern.shape[0]
    group_count = lax.axis_size("shard")
    local_rows = embeddings.shape[0]
    capacity = 2 * local_rows // group_count
    features = embeddings.shape[1]
    unit_rows = (
        embeddings * lax.rsqrt(jnp.sum(embeddings * embeddings, axis=1, keepdims=True) + 1e-06)
    ).astype(jnp.bfloat16)
    target_group = assign[labels]
    one_hot = (target_group[:, None] == jnp.arange(group_count, dtype=jnp.int32)[None, :]).astype(
        jnp.int32
    )
    earlier = jnp.cumsum(one_hot, axis=0) - one_hot
    send_slot = target_group * capacity + jnp.sum(earlier * one_hot, axis=1)
    doc_codes = labels * count + doc_block
    outgoing = (
        jnp.zeros((group_count * capacity, features), jnp.bfloat16).at[send_slot].set(unit_rows)
    )
    outgoing_codes = jnp.full((group_count * capacity,), -1, jnp.int32).at[send_slot].set(doc_codes)
    arrived, arrived_codes = (
        lax.all_to_all(outgoing, "shard", split_axis=0, concat_axis=0, tiled=True),
        lax.all_to_all(outgoing_codes, "shard", split_axis=0, concat_axis=0, tiled=True),
    )
    masks = row_masks(arrived_codes, pattern)
    row_count = arrived.shape[0]
    position = jnp.arange(row_count, dtype=jnp.int32)
    start_value = jnp.full((row_count,), -1.0, jnp.float32)
    columns = from_members(arrived)
    column_codes = from_members(arrived_codes)
    similarity = scores(arrived, columns)
    permitted_pairs = allowed(arrived_codes, masks, column_codes, count)
    column_position = jnp.arange(columns.shape[0], dtype=jnp.int32)
    permitted_pairs = permitted_pairs & (position[:, None] != column_position[None, :])
    best_match = jnp.maximum(
        start_value, jnp.max(jnp.where(permitted_pairs, similarity, -1.0), axis=1)
    )
    returned_max = lax.all_to_all(best_match, "shard", split_axis=0, concat_axis=0, tiled=True)
    return returned_max[send_slot]


def dot_nt(left, right):
    return lax.dot_general(left, right, (((1,), (1,)), ((), ())), preferred_element_type=F32)


def pack_kernel(
    groups, chips, first, slots, count, emb_ref, label_ref, block_ref, assign_ref, out_ref, slot_ref
):
    docs, features = emb_ref.shape
    labels = label_ref[...]
    clusters = assign_ref.shape[0] * assign_ref.shape[1]
    assign = assign_ref[...]

    group = jnp.zeros((1, docs), jnp.int32)
    start = jnp.zeros((1, docs), jnp.int32)
    stop = jnp.full((1, docs), clusters, jnp.int32)
    for g in range(1, groups):
        bound = jnp.sum((assign < g).astype(F32), axis=0, keepdims=True)
        bound = jnp.sum(bound, axis=1, keepdims=True).astype(jnp.int32)
        inside = labels >= bound
        group = group + inside.astype(jnp.int32)
        start = jnp.where(inside, jnp.maximum(start, bound), start)
        stop = jnp.where(inside, stop, jnp.minimum(stop, bound))
    extent = (stop - start).astype(F32)

    def home_of(cluster):
        above = ((cluster - start + 1) * chips - 1).astype(F32)
        return jnp.floor((above + 0.5) / extent).astype(jnp.int32)

    home = home_of(labels)
    beside = jnp.where(labels + 1 < stop, home_of(labels + 1), home)

    chip_id = lax.broadcasted_iota(jnp.int32, (chips, docs), 0)
    member = (chip_id == home) | (chip_id == beside)
    earlier = (
        lax.broadcasted_iota(jnp.int32, (docs, docs), 0)
        < lax.broadcasted_iota(jnp.int32, (docs, docs), 1)
    ).astype(F32).astype(BF16)
    rank = jnp.dot(
        member.astype(F32).astype(BF16), earlier, preferred_element_type=F32
    ).astype(jnp.int32) - first
    most = jnp.max(jnp.where(member, rank, -1), axis=0, keepdims=True)
    most = jnp.max(most, axis=1, keepdims=True)
    past = jnp.where(most >= slots - 1, 1.0, 0.0) + jnp.where(most >= slots + MORE - 2, 1.0, 0.0)
    slot = jnp.where(member & (rank >= 0) & (rank < slots - 1), rank, -1)
    slot_ref[...] = slot

    code = (labels + group) * count + block_ref[...] + 1
    row_id = lax.broadcasted_iota(jnp.int32, (8, docs), 0)
    digits = jnp.where(row_id == 0, code >> 7, jnp.where(row_id == 1, code & 127, 0))
    digits = digits.astype(F32).astype(BF16)

    slot_id = lax.broadcasted_iota(jnp.int32, (chips, slots, docs), 1)
    picks = (slot_id == slot[:, None, :]).astype(F32).reshape(chips * slots, docs).astype(BF16)

    lane_slot = lax.broadcasted_iota(jnp.int32, (LANES, docs), 0)
    code_rows = []
    for chip in range(chips):
        pick = (lane_slot == slot[chip : chip + 1, :]).astype(F32).astype(BF16)
        sent = dot_nt(digits, pick)
        row = [sent[0:1, :], sent[1:2, :], jnp.broadcast_to(past, (1, LANES))]
        row.append(jnp.zeros((1, features - 3 * LANES), F32))
        code_rows.append(jnp.concatenate(row, axis=1))
    code_rows = jnp.concatenate(code_rows, axis=0)

    emb = emb_ref[...]
    unit = (emb * lax.rsqrt(jnp.sum(emb * emb, axis=1, keepdims=True) + 1e-06)).astype(BF16)
    step = min(features, 4 * LANES)
    last = lax.broadcasted_iota(jnp.int32, (chips, slots, step), 1) == slots - 1
    for at in range(0, features, step):
        rows = jnp.dot(picks, unit[:, at : at + step], preferred_element_type=F32)
        rows = rows.reshape(chips, slots, step)
        rows = jnp.where(last, code_rows[:, None, at : at + step], rows)
        out_ref[:, at : at + step] = rows.reshape(chips * slots, step).astype(BF16)


def codes_of(rows_ref, chips, segments, count):
    rows = rows_ref.shape[0]
    slots = sum(segments)
    at_row = lax.broadcasted_iota(jnp.int32, (chips, rows), 1)
    chip_row = lax.broadcasted_iota(jnp.int32, (chips, rows), 0) * slots
    found, begin = [], 0
    for length in segments:
        pick = (at_row == chip_row + (begin + length - 1)).astype(F32).astype(BF16)
        sent = jnp.dot(pick, rows_ref[:, : 2 * LANES], preferred_element_type=F32)
        found.append(sent[:, :LANES] * 128.0 + sent[:, LANES:])
        begin += length
    pieces = []
    for chip in range(chips):
        for length, code in zip(segments, found):
            pieces.append(code[chip : chip + 1, :length])
    code = jnp.concatenate(pieces, axis=1) - 1.0
    label = jnp.floor((code + 0.5) / count)
    block = jnp.where(code < 0.0, -1.0, code - label * count)
    return jnp.where(code < 0.0, -8.0, label), block


def down(row):
    return jnp.transpose(jnp.broadcast_to(row, (8, row.shape[1])))[:, 0:1]


def hot_blocks(block):
    lane = lax.broadcasted_iota(jnp.int32, (block.shape[0], LANES), 1).astype(F32)
    return (lane == block).astype(F32).astype(BF16)


def match_rows(left_ref, row_label, row_terms, right_ref, label, hot, same, best):
    rows, columns = left_ref.shape[0], right_ref.shape[0]
    row_at = lax.broadcasted_iota(jnp.int32, (rows, LANES), 0)
    col_at = lax.broadcasted_iota(jnp.int32, (rows, LANES), 1)
    left = left_ref[...]
    step = 2 * LANES
    for at in range(0, columns, step):
        width = min(step, columns - at)
        sim = dot_nt(left, right_ref[at : at + width, :])
        sim += dot_nt(row_terms, hot[at : at + width, :])
        for piece in range(0, width, LANES):
            span = min(LANES, width - piece)
            near = jnp.abs(row_label[:, :span] - label[:, at + piece : at + piece + span]) <= 1.0
            if same:
                near = near & (row_at[:, :span] != col_at[:, :span] + (at + piece))
            value = jnp.where(near, sim[:, piece : piece + span], -1.0)
            if span < LANES:
                value = jnp.concatenate([value, jnp.full((rows, LANES - span), -1.0, F32)], axis=1)
            best = jnp.maximum(best, value)
    return best


def match_own_kernel(
    chips, segments, own_ref, pattern_ref, best_ref, label_ref, terms_ref
):
    rows = own_ref.shape[0]
    count = pattern_ref.shape[0]
    label, block = codes_of(own_ref, chips, segments, count)
    hot = hot_blocks(down(block))
    table = jnp.zeros((LANES, LANES), F32)
    from_block = lax.broadcasted_iota(jnp.int32, (LANES, LANES), 0)
    to_block = lax.broadcasted_iota(jnp.int32, (LANES, LANES), 1)
    for a in range(count):
        for b in range(count):
            term = BARRED * (pattern_ref[a, b].astype(F32) - 1.0)
            table = jnp.where((from_block == a) & (to_block == b), term, table)
    row_terms = jnp.dot(hot, table.astype(BF16), preferred_element_type=F32).astype(BF16)
    row_label = jnp.broadcast_to(down(label), (rows, LANES))
    label_ref[...] = row_label
    terms_ref[...] = row_terms
    best = jnp.full((rows, LANES), -1.0, F32)
    best_ref[...] = match_rows(own_ref, row_label, row_terms, own_ref, label, hot, True, best)


def match_other_kernel(
    chips, segments, count, own_ref, other_ref, before_ref, label_ref, terms_ref, best_ref
):
    slots = sum(segments)
    label, block = codes_of(other_ref, chips, segments, count)
    hot = hot_blocks(down(block))
    best = match_rows(
        own_ref, label_ref[...], terms_ref[...], other_ref, label, hot, False, before_ref[...]
    )
    across = jnp.max(jnp.transpose(best), axis=0, keepdims=True)
    for chip in range(chips):
        best_ref[chip : chip + 1, 0:slots] = across[:, chip * slots : (chip + 1) * slots]


def unpack_kernel(chips, slots, back_ref, slot_ref, out_ref):
    docs = slot_ref.shape[1]
    back = jnp.transpose(back_ref[...])
    slot_id = lax.broadcasted_iota(jnp.int32, (slots, docs), 0)
    best = jnp.full((slots, docs), -1.0, F32)
    for chip in range(chips):
        here = slot_id == slot_ref[chip : chip + 1, :]
        best = jnp.maximum(best, jnp.where(here, back[0:slots, chip : chip + 1], -1.0))
    out_ref[...] = jnp.max(best, axis=0, keepdims=True)


def in_vmem():
    return pl.BlockSpec(memory_space=pltpu.VMEM)


def in_smem():
    return pl.BlockSpec(memory_space=pltpu.SMEM)


def params():
    return pltpu.CompilerParams(vmem_limit_bytes=VMEM_LIMIT)


def cost(flops, moved):
    return pl.CostEstimate(flops=flops, bytes_accessed=moved, transcendentals=0)


def send(embeddings, labels, doc_block, assign, count, first, slots):
    groups = lax.axis_size("shard")
    chips = groups * lax.axis_size("grp")
    docs, features = embeddings.shape
    outgoing, slot = pl.pallas_call(
        functools.partial(pack_kernel, groups, chips, first, slots, count),
        out_shape=(
            jax.ShapeDtypeStruct((chips * slots, features), BF16),
            jax.ShapeDtypeStruct((chips, docs), jnp.int32),
        ),
        in_specs=[in_vmem()] * 4,
        out_specs=(in_vmem(), in_vmem()),
        compiler_params=params(),
        name="pack",
    )(
        embeddings,
        labels.reshape(1, docs),
        doc_block.reshape(1, docs),
        assign.reshape(-1, LANES),
    )
    arrived = lax.all_to_all(
        outgoing, ("shard", "grp"), split_axis=0, concat_axis=0, tiled=True
    )
    return arrived, slot


def match(arrived, slot, pattern, segments):
    chips, docs = slot.shape
    slots = sum(segments)
    rows, features = arrived.shape
    cores = lax.axis_size("sub")
    other = lax.ppermute(arrived, "sub", [(i, (i + 1) % cores) for i in range(cores)])
    work = cost(2 * rows * rows * features, 2 * rows * features)
    best, label, terms = pl.pallas_call(
        functools.partial(match_own_kernel, chips, segments),
        out_shape=(
            jax.ShapeDtypeStruct((rows, LANES), F32),
            jax.ShapeDtypeStruct((rows, LANES), F32),
            jax.ShapeDtypeStruct((rows, LANES), BF16),
        ),
        in_specs=[in_vmem(), in_smem()],
        out_specs=(in_vmem(), in_vmem(), in_vmem()),
        compiler_params=params(),
        cost_estimate=work,
        name="match_own",
    )(arrived, pattern)
    best = pl.pallas_call(
        functools.partial(match_other_kernel, chips, segments, pattern.shape[0]),
        out_shape=jax.ShapeDtypeStruct((chips, LANES), F32),
        in_specs=[in_vmem()] * 5,
        out_specs=in_vmem(),
        compiler_params=params(),
        cost_estimate=work,
        name="match_other",
    )(arrived, other, best, label, terms)
    back = lax.all_to_all(best, ("shard", "grp"), split_axis=0, concat_axis=0, tiled=True)
    return pl.pallas_call(
        functools.partial(unpack_kernel, chips, slots),
        out_shape=jax.ShapeDtypeStruct((1, docs), F32),
        in_specs=[in_vmem()] * 2,
        out_specs=in_vmem(),
        compiler_params=params(),
        name="unpack",
    )(back, slot).reshape(docs)


def per_device(embeddings, labels, doc_block, assign, pattern):
    chips = lax.axis_size("shard") * lax.axis_size("grp")
    docs, features = embeddings.shape
    count = pattern.shape[0]
    mean = docs // chips
    slots = -(-(mean + int(3 * math.sqrt(mean))) // 8) * 8
    inputs = (embeddings, labels, doc_block, assign)

    arrived, slot = send(*inputs, count, 0, slots)
    found = match(arrived, slot, pattern, (slots,))

    past = arrived.reshape(chips, slots, features)[:, slots - 1, 2 * LANES : 3 * LANES]
    past = jnp.max(past.astype(F32), axis=0, keepdims=True)
    for axis in ("sub", "parts"):
        size = lax.axis_size(axis)
        for shift in range(1, size):
            to = [(i, (i + shift) % size) for i in range(size)]
            past = jnp.maximum(past, lax.ppermute(past, axis, to))

    def second_round():
        more, more_slot = send(*inputs, count, slots - 1, MORE)
        both = jnp.concatenate(
            [arrived.reshape(chips, slots, features), more.reshape(chips, MORE, features)], axis=1
        ).reshape(chips * (slots + MORE), features)
        both_slot = jnp.where(more_slot >= 0, more_slot + slots, slot)
        return match(both, both_slot, pattern, (slots, MORE))

    return lax.cond(
        past[0, 0] > 0.0,
        lambda: lax.cond(
            past[0, 0] > 1.0, lambda: general_form(*inputs, pattern), second_round
        ),
        lambda: found,
    )


def solution(mesh):
    in_specs = (
        P(("parts", "shard", "grp", "sub"), None),
        P(("parts", "shard", "grp", "sub")),
        P(("parts", "shard", "grp", "sub")),
        P("parts"),
        P(),
    )
    out_specs = P(("parts", "shard", "grp", "sub"))
    return jax.shard_map(
        per_device, mesh=mesh, in_specs=in_specs, out_specs=out_specs, check_vma=False
    )
```

```python
import functools
import math

import jax
import jax.numpy as jnp
from jax import lax
from jax.experimental import pallas as pl
from jax.experimental.pallas import tpu as pltpu
from jax.sharding import PartitionSpec as P

BF16 = jnp.bfloat16
F32 = jnp.float32
VMEM_LIMIT = 32 * 1024 * 1024
LANES = 128
PIECES = 2
MORE = (16, 40)


def row_masks(doc_codes, pattern):
    count = pattern.shape[0]
    powers = jnp.left_shift(jnp.int32(1), jnp.arange(count, dtype=jnp.int32))
    pattern_bits = jnp.sum(pattern * powers[None, :], axis=1)
    block_ids = doc_codes % count
    picked = block_ids[:, None] == jnp.arange(count, dtype=jnp.int32)[None, :]
    return jnp.sum(jnp.where(picked, pattern_bits[None, :], 0), axis=1)


def allowed(row_codes, masks, col_codes, count):
    adjacent = jnp.abs(row_codes[:, None] // count - col_codes[None, :] // count) <= 1
    filled = (col_codes >= 0)[None, :]
    permitted = jnp.right_shift(masks[:, None], col_codes[None, :] % count) % 2 == 1
    return adjacent & filled & permitted


def scores(left_rows, right_rows):
    return lax.dot_general(
        left_rows, right_rows, (((1,), (1,)), ((), ())), preferred_element_type=jnp.float32
    )


def from_members(rows):
    members = lax.axis_size(("grp", "sub"))
    shifts = [[(i, (i + shift) % members) for i in range(members)] for shift in range(1, members)]
    return jnp.concatenate([rows] + [lax.ppermute(rows, ("grp", "sub"), to) for to in shifts])


def general_form(embeddings, labels, doc_block, assign, pattern):
    count = pattern.shape[0]
    group_count = lax.axis_size("shard")
    local_rows = embeddings.shape[0]
    capacity = 2 * local_rows // group_count
    features = embeddings.shape[1]
    unit_rows = (
        embeddings * lax.rsqrt(jnp.sum(embeddings * embeddings, axis=1, keepdims=True) + 1e-06)
    ).astype(jnp.bfloat16)
    target_group = assign[labels]
    one_hot = (target_group[:, None] == jnp.arange(group_count, dtype=jnp.int32)[None, :]).astype(
        jnp.int32
    )
    earlier = jnp.cumsum(one_hot, axis=0) - one_hot
    send_slot = target_group * capacity + jnp.sum(earlier * one_hot, axis=1)
    doc_codes = labels * count + doc_block
    outgoing = (
        jnp.zeros((group_count * capacity, features), jnp.bfloat16).at[send_slot].set(unit_rows)
    )
    outgoing_codes = jnp.full((group_count * capacity,), -1, jnp.int32).at[send_slot].set(doc_codes)
    arrived, arrived_codes = (
        lax.all_to_all(outgoing, "shard", split_axis=0, concat_axis=0, tiled=True),
        lax.all_to_all(outgoing_codes, "shard", split_axis=0, concat_axis=0, tiled=True),
    )
    masks = row_masks(arrived_codes, pattern)
    row_count = arrived.shape[0]
    position = jnp.arange(row_count, dtype=jnp.int32)
    start_value = jnp.full((row_count,), -1.0, jnp.float32)
    columns = from_members(arrived)
    column_codes = from_members(arrived_codes)
    similarity = scores(arrived, columns)
    permitted_pairs = allowed(arrived_codes, masks, column_codes, count)
    column_position = jnp.arange(columns.shape[0], dtype=jnp.int32)
    permitted_pairs = permitted_pairs & (position[:, None] != column_position[None, :])
    best_match = jnp.maximum(
        start_value, jnp.max(jnp.where(permitted_pairs, similarity, -1.0), axis=1)
    )
    returned_max = lax.all_to_all(best_match, "shard", split_axis=0, concat_axis=0, tiled=True)
    return returned_max[send_slot]


def dot_nt(left, right):
    return lax.dot_general(left, right, (((1,), (1,)), ((), ())), preferred_element_type=F32)


def pack_kernel(
    groups, chips, first, slots, count, emb_hbm, label_hbm, block_hbm, assign_hbm, out_ref,
    slot_ref, emb_ref, label_ref, block_ref, assign_ref, unit_ref, copied,
):
    docs, features = emb_hbm.shape
    step = docs // PIECES
    small = [(label_hbm, label_ref), (assign_hbm, assign_ref), (block_hbm, block_ref)]
    moves = list(small)
    for piece in range(PIECES):
        rows = pl.ds(piece * step, step)
        moves.append((emb_hbm.at[rows], emb_ref.at[rows]))
    copies = [
        pltpu.make_async_copy(source, target, copied.at[i])
        for i, (source, target) in enumerate(moves)
    ]
    for copy in copies:
        copy.start()
    for copy in copies[: len(small)]:
        copy.wait()
    labels = label_ref[...]
    clusters = assign_ref.shape[0] * assign_ref.shape[1]
    assign = assign_ref[...]

    group = jnp.zeros((1, docs), jnp.int32)
    start = jnp.zeros((1, docs), jnp.int32)
    stop = jnp.full((1, docs), clusters, jnp.int32)
    for g in range(1, groups):
        bound = jnp.sum((assign < g).astype(F32), axis=0, keepdims=True)
        bound = jnp.sum(bound, axis=1, keepdims=True).astype(jnp.int32)
        inside = labels >= bound
        group = group + inside.astype(jnp.int32)
        start = jnp.where(inside, jnp.maximum(start, bound), start)
        stop = jnp.where(inside, stop, jnp.minimum(stop, bound))
    extent = (stop - start).astype(F32)

    def home_of(cluster):
        above = ((cluster - start + 1) * chips - 1).astype(F32)
        return jnp.floor((above + 0.5) / extent).astype(jnp.int32)

    home = home_of(labels)
    beside = jnp.where(labels + 1 < stop, home_of(labels + 1), home)

    chip_id = lax.broadcasted_iota(jnp.int32, (chips, docs), 0)
    member = (chip_id == home) | (chip_id == beside)
    earlier = (
        lax.broadcasted_iota(jnp.int32, (docs, docs), 0)
        < lax.broadcasted_iota(jnp.int32, (docs, docs), 1)
    ).astype(F32).astype(BF16)
    rank = jnp.dot(
        member.astype(F32).astype(BF16), earlier, preferred_element_type=F32
    ).astype(jnp.int32) - first
    most = jnp.max(jnp.where(member, rank, -1), axis=0, keepdims=True)
    most = jnp.max(most, axis=1, keepdims=True)
    past = jnp.where(most >= slots - 1, 1.0, 0.0)
    for more in MORE:
        past = past + jnp.where(most >= slots + more - 2, 1.0, 0.0)
    slot = jnp.where(member & (rank >= 0) & (rank < slots - 1), rank, -1)
    slot_ref[...] = slot

    code = (labels + group + 2) * count + block_ref[...] + 1
    row_id = lax.broadcasted_iota(jnp.int32, (8, docs), 0)
    digits = jnp.where(row_id == 0, code >> 7, jnp.where(row_id == 1, code & 127, 0))
    digits = digits.astype(F32).astype(BF16)

    slot_id = lax.broadcasted_iota(jnp.int32, (chips, slots, docs), 1)
    picks = (slot_id == slot[:, None, :]).astype(F32).reshape(chips * slots, docs).astype(BF16)

    sent = dot_nt(digits, picks)
    tail = lax.broadcasted_iota(jnp.int32, (8, 3 * LANES), 0) == 7
    fill = jnp.zeros((1, LANES - slots), F32)
    for piece, copy in enumerate(copies[len(small) :]):
        copy.wait()
        rows = slice(piece * step, (piece + 1) * step)
        emb = emb_ref[rows, :]
        scale = lax.rsqrt(jnp.sum(emb * emb, axis=1, keepdims=True) + 1e-06)
        unit_ref[rows, :] = (emb * scale).astype(BF16)
    step = min(features, 4 * LANES)
    for at in range(0, features, step):
        rows = jnp.dot(picks, unit_ref[:, at : at + step], preferred_element_type=F32)
        out_ref[:, at : at + step] = rows.astype(BF16)
    for chip in range(chips):
        here = slice(chip * slots, (chip + 1) * slots)
        row = [sent[0:1, here], fill, sent[1:2, here], fill, jnp.broadcast_to(past, (1, LANES))]
        end = (chip + 1) * slots
        held = out_ref[end - 8 : end, : 3 * LANES].astype(F32)
        held = jnp.where(tail, jnp.concatenate(row, axis=1), held)
        out_ref[end - 8 : end, : 3 * LANES] = held.astype(BF16)


def codes_of(rows_ref, chips, segments):
    slots = sum(segments)
    pieces = []
    for chip in range(chips):
        end = chip * slots
        for length in segments:
            end += length
            sent = rows_ref[end - 8 : end, : 2 * LANES].astype(F32)[7:8, :]
            pieces.append((sent[:, :LANES] * 128.0 + sent[:, LANES:])[:, :length])
    return jnp.concatenate(pieces, axis=1).astype(jnp.int32)


def match_rows(left_ref, row_base, row_bits, right_ref, code, same, best):
    rows, columns = left_ref.shape[0], right_ref.shape[0]
    apart = lax.broadcasted_iota(jnp.int32, (rows, LANES), 0) - lax.broadcasted_iota(
        jnp.int32, (rows, LANES), 1
    )
    left = left_ref[...]
    step = 2 * LANES
    for at in range(0, columns, step):
        width = min(step, columns - at)
        sim = dot_nt(left, right_ref[at : at + width, :])
        for piece in range(0, width, LANES):
            span = min(LANES, width - piece)
            begin = at + piece
            gap = code[:, begin : begin + span] - row_base[:, :span]
            gap = jnp.minimum(jnp.maximum(gap, 0), 31)
            fits = jnp.left_shift(row_bits[:, :span], gap) < 0
            if same:
                fits = fits & (apart[:, :span] != begin)
            value = jnp.where(fits, sim[:, piece : piece + span], -1.0)
            if span < LANES:
                value = jnp.concatenate([value, jnp.full((rows, LANES - span), -1.0, F32)], axis=1)
            best = jnp.maximum(best, value)
    return best


def match_own_kernel(chips, segments, own_ref, pattern_ref, best_ref, base_ref, bits_ref):
    rows = own_ref.shape[0]
    count = pattern_ref.shape[0]
    code = codes_of(own_ref, chips, segments)
    label = jnp.floor((code.astype(F32) - 0.5) / count).astype(jnp.int32)
    block = code - 1 - label * count
    base = count * (label - 1)
    bits = jnp.zeros_like(code)
    for a in range(count):
        word = 0
        for b in range(count):
            for turn in range(3):
                word += pattern_ref[a, b] << (30 - turn * count - b)
        bits = jnp.where(block == a, word, bits)
    bits = jnp.where(code == 0, 0, bits)
    both = jnp.concatenate([base, bits, jnp.zeros((6, rows), jnp.int32)], axis=0)
    both = jnp.transpose(both)
    row_base = jnp.broadcast_to(both[:, 0:1], (rows, LANES))
    row_bits = jnp.broadcast_to(both[:, 1:2], (rows, LANES))
    base_ref[...] = row_base
    bits_ref[...] = row_bits
    best = jnp.full((rows, LANES), -1.0, F32)
    best_ref[...] = match_rows(own_ref, row_base, row_bits, own_ref, code, True, best)


def match_other_kernel(
    chips, segments, own_ref, other_ref, before_ref, base_ref, bits_ref, best_ref
):
    slots = sum(segments)
    code = codes_of(other_ref, chips, segments)
    best = match_rows(
        own_ref, base_ref[...], bits_ref[...], other_ref, code, False, before_ref[...]
    )
    across = jnp.max(jnp.transpose(best), axis=0, keepdims=True)
    for chip in range(chips):
        best_ref[chip : chip + 1, 0:slots] = across[:, chip * slots : (chip + 1) * slots]


def unpack_kernel(chips, slots, back_ref, slot_ref, out_ref):
    docs = slot_ref.shape[1]
    back = jnp.transpose(back_ref[...])
    slot_id = lax.broadcasted_iota(jnp.int32, (slots, docs), 0)
    best = jnp.full((slots, docs), -1.0, F32)
    for chip in range(chips):
        here = slot_id == slot_ref[chip : chip + 1, :]
        best = jnp.maximum(best, jnp.where(here, back[0:slots, chip : chip + 1], -1.0))
    out_ref[...] = jnp.max(best, axis=0, keepdims=True)


def in_vmem():
    return pl.BlockSpec(memory_space=pltpu.VMEM)


def in_smem():
    return pl.BlockSpec(memory_space=pltpu.SMEM)


def params():
    return pltpu.CompilerParams(vmem_limit_bytes=VMEM_LIMIT)


def cost(flops, moved):
    return pl.CostEstimate(flops=flops, bytes_accessed=moved, transcendentals=0)


def send(embeddings, labels, doc_block, assign, count, first, slots):
    groups = lax.axis_size("shard")
    chips = groups * lax.axis_size("grp")
    docs, features = embeddings.shape
    outgoing, slot = pl.pallas_call(
        functools.partial(pack_kernel, groups, chips, first, slots, count),
        out_shape=(
            jax.ShapeDtypeStruct((chips * slots, features), BF16),
            jax.ShapeDtypeStruct((chips, docs), jnp.int32),
        ),
        in_specs=[pl.BlockSpec(memory_space=pl.ANY)] * 4,
        out_specs=(in_vmem(), in_vmem()),
        scratch_shapes=[
            pltpu.VMEM((docs, features), F32),
            pltpu.VMEM((1, docs), jnp.int32),
            pltpu.VMEM((1, docs), jnp.int32),
            pltpu.VMEM((assign.shape[0] // LANES, LANES), jnp.int32),
            pltpu.VMEM((docs, features), BF16),
            pltpu.SemaphoreType.DMA((3 + PIECES,)),
        ],
        compiler_params=params(),
        name="pack",
    )(
        embeddings,
        labels.reshape(1, docs),
        doc_block.reshape(1, docs),
        assign.reshape(-1, LANES),
    )
    arrived = lax.all_to_all(
        outgoing, ("shard", "grp"), split_axis=0, concat_axis=0, tiled=True
    )
    return arrived, slot


def match(arrived, slot, pattern, segments):
    chips, docs = slot.shape
    slots = sum(segments)
    rows, features = arrived.shape
    cores = lax.axis_size("sub")
    other = lax.ppermute(arrived, "sub", [(i, (i + 1) % cores) for i in range(cores)])
    work = cost(2 * rows * rows * features, 2 * rows * features)
    best, base, bits = pl.pallas_call(
        functools.partial(match_own_kernel, chips, segments),
        out_shape=(
            jax.ShapeDtypeStruct((rows, LANES), F32),
            jax.ShapeDtypeStruct((rows, LANES), jnp.int32),
            jax.ShapeDtypeStruct((rows, LANES), jnp.int32),
        ),
        in_specs=[in_vmem(), in_smem()],
        out_specs=(in_vmem(), in_vmem(), in_vmem()),
        compiler_params=params(),
        cost_estimate=work,
        name="match_own",
    )(arrived, pattern)
    best = pl.pallas_call(
        functools.partial(match_other_kernel, chips, segments),
        out_shape=jax.ShapeDtypeStruct((chips, LANES), F32),
        in_specs=[in_vmem()] * 5,
        out_specs=in_vmem(),
        compiler_params=params(),
        cost_estimate=work,
        name="match_other",
    )(arrived, other, best, base, bits)
    back = lax.all_to_all(best, ("shard", "grp"), split_axis=0, concat_axis=0, tiled=True)
    return pl.pallas_call(
        functools.partial(unpack_kernel, chips, slots),
        out_shape=jax.ShapeDtypeStruct((1, docs), F32),
        in_specs=[in_vmem()] * 2,
        out_specs=in_vmem(),
        compiler_params=params(),
        name="unpack",
    )(back, slot).reshape(docs)


def per_device(embeddings, labels, doc_block, assign, pattern):
    chips = lax.axis_size("shard") * lax.axis_size("grp")
    docs, features = embeddings.shape
    count = pattern.shape[0]
    mean = docs // chips
    slots = -(-(mean + int(3 * math.sqrt(mean))) // 8) * 8
    inputs = (embeddings, labels, doc_block, assign)

    arrived, slot = send(*inputs, count, 0, slots)
    found = match(arrived, slot, pattern, (slots,))

    past = arrived.reshape(chips, slots, features)[:, slots - 1, 2 * LANES : 3 * LANES]
    past = jnp.max(past.astype(F32), axis=0, keepdims=True)
    for axis in ("sub", "parts"):
        size = lax.axis_size(axis)
        for shift in range(1, size):
            to = [(i, (i + shift) % size) for i in range(size)]
            past = jnp.maximum(past, lax.ppermute(past, axis, to))

    def second_round(size):
        more, more_slot = send(*inputs, count, slots - 1, size)
        both = jnp.concatenate(
            [arrived.reshape(chips, slots, features), more.reshape(chips, size, features)], axis=1
        ).reshape(chips * (slots + size), features)
        both_slot = jnp.where(more_slot >= 0, more_slot + slots, slot)
        return match(both, both_slot, pattern, (slots, size))

    def in_rounds(level):
        if level > len(MORE):
            return general_form(*inputs, pattern)
        return lax.cond(
            past[0, 0] > level,
            lambda: in_rounds(level + 1),
            lambda: second_round(MORE[level - 1]) if level else found,
        )

    return in_rounds(0)


def solution(mesh):
    in_specs = (
        P(("parts", "shard", "grp", "sub"), None),
        P(("parts", "shard", "grp", "sub")),
        P(("parts", "shard", "grp", "sub")),
        P("parts"),
        P(),
    )
    out_specs = P(("parts", "shard", "grp", "sub"))
    return jax.shard_map(
        per_device, mesh=mesh, in_specs=in_specs, out_specs=out_specs, check_vma=False
    )
```

```python
import functools
import math

import jax
import jax.numpy as jnp
from jax import lax
from jax.experimental import pallas as pl
from jax.experimental.pallas import tpu as pltpu
from jax.sharding import PartitionSpec as P

BF16 = jnp.bfloat16
F32 = jnp.float32
VMEM_LIMIT = 32 * 1024 * 1024
LANES = 128
PIECES = 2
MORE = (24, 40)


def row_masks(doc_codes, pattern):
    count = pattern.shape[0]
    powers = jnp.left_shift(jnp.int32(1), jnp.arange(count, dtype=jnp.int32))
    pattern_bits = jnp.sum(pattern * powers[None, :], axis=1)
    block_ids = doc_codes % count
    picked = block_ids[:, None] == jnp.arange(count, dtype=jnp.int32)[None, :]
    return jnp.sum(jnp.where(picked, pattern_bits[None, :], 0), axis=1)


def allowed(row_codes, masks, col_codes, count):
    adjacent = jnp.abs(row_codes[:, None] // count - col_codes[None, :] // count) <= 1
    filled = (col_codes >= 0)[None, :]
    permitted = jnp.right_shift(masks[:, None], col_codes[None, :] % count) % 2 == 1
    return adjacent & filled & permitted


def scores(left_rows, right_rows):
    return lax.dot_general(
        left_rows, right_rows, (((1,), (1,)), ((), ())), preferred_element_type=jnp.float32
    )


def from_members(rows):
    members = lax.axis_size(("grp", "sub"))
    shifts = [[(i, (i + shift) % members) for i in range(members)] for shift in range(1, members)]
    return jnp.concatenate([rows] + [lax.ppermute(rows, ("grp", "sub"), to) for to in shifts])


def general_form(embeddings, labels, doc_block, assign, pattern):
    count = pattern.shape[0]
    group_count = lax.axis_size("shard")
    local_rows = embeddings.shape[0]
    capacity = 2 * local_rows // group_count
    features = embeddings.shape[1]
    unit_rows = (
        embeddings * lax.rsqrt(jnp.sum(embeddings * embeddings, axis=1, keepdims=True) + 1e-06)
    ).astype(jnp.bfloat16)
    target_group = assign[labels]
    one_hot = (target_group[:, None] == jnp.arange(group_count, dtype=jnp.int32)[None, :]).astype(
        jnp.int32
    )
    earlier = jnp.cumsum(one_hot, axis=0) - one_hot
    send_slot = target_group * capacity + jnp.sum(earlier * one_hot, axis=1)
    doc_codes = labels * count + doc_block
    outgoing = (
        jnp.zeros((group_count * capacity, features), jnp.bfloat16).at[send_slot].set(unit_rows)
    )
    outgoing_codes = jnp.full((group_count * capacity,), -1, jnp.int32).at[send_slot].set(doc_codes)
    arrived, arrived_codes = (
        lax.all_to_all(outgoing, "shard", split_axis=0, concat_axis=0, tiled=True),
        lax.all_to_all(outgoing_codes, "shard", split_axis=0, concat_axis=0, tiled=True),
    )
    masks = row_masks(arrived_codes, pattern)
    row_count = arrived.shape[0]
    position = jnp.arange(row_count, dtype=jnp.int32)
    start_value = jnp.full((row_count,), -1.0, jnp.float32)
    columns = from_members(arrived)
    column_codes = from_members(arrived_codes)
    similarity = scores(arrived, columns)
    permitted_pairs = allowed(arrived_codes, masks, column_codes, count)
    column_position = jnp.arange(columns.shape[0], dtype=jnp.int32)
    permitted_pairs = permitted_pairs & (position[:, None] != column_position[None, :])
    best_match = jnp.maximum(
        start_value, jnp.max(jnp.where(permitted_pairs, similarity, -1.0), axis=1)
    )
    returned_max = lax.all_to_all(best_match, "shard", split_axis=0, concat_axis=0, tiled=True)
    return returned_max[send_slot]


def dot_nt(left, right):
    return lax.dot_general(left, right, (((1,), (1,)), ((), ())), preferred_element_type=F32)


def pack_kernel(
    groups, chips, first, slots, count, emb_hbm, label_hbm, block_hbm, assign_hbm, out_ref,
    slot_ref, emb_ref, label_ref, block_ref, assign_ref, unit_ref, copied,
):
    docs, features = emb_hbm.shape
    step = docs // PIECES
    small = [(label_hbm, label_ref), (assign_hbm, assign_ref), (block_hbm, block_ref)]
    moves = list(small)
    for piece in range(PIECES):
        rows = pl.ds(piece * step, step)
        moves.append((emb_hbm.at[rows], emb_ref.at[rows]))
    copies = [
        pltpu.make_async_copy(source, target, copied.at[i])
        for i, (source, target) in enumerate(moves)
    ]
    for copy in copies:
        copy.start()
    for copy in copies[: len(small)]:
        copy.wait()
    labels = label_ref[...]
    clusters = assign_ref.shape[0] * assign_ref.shape[1]
    assign = assign_ref[...]

    group = jnp.zeros((1, docs), jnp.int32)
    start = jnp.zeros((1, docs), jnp.int32)
    stop = jnp.full((1, docs), clusters, jnp.int32)
    for g in range(1, groups):
        bound = jnp.sum((assign < g).astype(F32), axis=0, keepdims=True)
        bound = jnp.sum(bound, axis=1, keepdims=True).astype(jnp.int32)
        inside = labels >= bound
        group = group + inside.astype(jnp.int32)
        start = jnp.where(inside, jnp.maximum(start, bound), start)
        stop = jnp.where(inside, stop, jnp.minimum(stop, bound))
    extent = (stop - start).astype(F32)

    def home_of(cluster):
        above = ((cluster - start + 1) * chips - 1).astype(F32)
        return jnp.floor((above + 0.5) / extent).astype(jnp.int32)

    home = home_of(labels)
    beside = jnp.where(labels + 1 < stop, home_of(labels + 1), home)

    chip_id = lax.broadcasted_iota(jnp.int32, (chips, docs), 0)
    member = (chip_id == home) | (chip_id == beside)
    earlier = (
        lax.broadcasted_iota(jnp.int32, (docs, docs), 0)
        < lax.broadcasted_iota(jnp.int32, (docs, docs), 1)
    ).astype(F32).astype(BF16)
    rank = jnp.dot(
        member.astype(F32).astype(BF16), earlier, preferred_element_type=F32
    ).astype(jnp.int32) - first
    most = jnp.max(jnp.where(member, rank, -1), axis=0, keepdims=True)
    most = jnp.max(most, axis=1, keepdims=True)
    past = jnp.where(most >= slots - 1, 1.0, 0.0)
    for more in MORE:
        past = past + jnp.where(most >= slots + more - 2, 1.0, 0.0)
    slot = jnp.where(member & (rank >= 0) & (rank < slots - 1), rank, -1)
    slot_ref[...] = slot

    code = (labels + group + 2) * count + block_ref[...] + 1
    row_id = lax.broadcasted_iota(jnp.int32, (8, docs), 0)
    digits = jnp.where(row_id == 0, code >> 7, jnp.where(row_id == 1, code & 127, 0))
    digits = digits.astype(F32).astype(BF16)

    slot_id = lax.broadcasted_iota(jnp.int32, (chips, slots, docs), 1)
    picks = (slot_id == slot[:, None, :]).astype(F32).reshape(chips * slots, docs).astype(BF16)

    sent = dot_nt(digits, picks)
    tail = lax.broadcasted_iota(jnp.int32, (8, 3 * LANES), 0) == 7
    fill = jnp.zeros((1, LANES - slots), F32)
    for piece, copy in enumerate(copies[len(small) :]):
        copy.wait()
        rows = slice(piece * step, (piece + 1) * step)
        emb = emb_ref[rows, :]
        scale = lax.rsqrt(jnp.sum(emb * emb, axis=1, keepdims=True) + 1e-06)
        unit_ref[rows, :] = (emb * scale).astype(BF16)
    step = min(features, 4 * LANES)
    for at in range(0, features, step):
        rows = jnp.dot(picks, unit_ref[:, at : at + step], preferred_element_type=F32)
        out_ref[:, at : at + step] = rows.astype(BF16)
    for chip in range(chips):
        here = slice(chip * slots, (chip + 1) * slots)
        row = [sent[0:1, here], fill, sent[1:2, here], fill, jnp.broadcast_to(past, (1, LANES))]
        end = (chip + 1) * slots
        held = out_ref[end - 8 : end, : 3 * LANES].astype(F32)
        held = jnp.where(tail, jnp.concatenate(row, axis=1), held)
        out_ref[end - 8 : end, : 3 * LANES] = held.astype(BF16)


def codes_of(rows_ref, chips):
    slots = rows_ref.shape[0] // chips
    pieces = []
    for end in range(slots, chips * slots + 1, slots):
        sent = rows_ref[end - 8 : end, : 2 * LANES].astype(F32)[7:8, :]
        pieces.append((sent[:, :LANES] * 128.0 + sent[:, LANES:])[:, :slots])
    return jnp.concatenate(pieces, axis=1).astype(jnp.int32)


def row_words(code, pattern_ref):
    rows = code.shape[1]
    count = pattern_ref.shape[0]
    label = jnp.floor((code.astype(F32) - 0.5) / count).astype(jnp.int32)
    block = code - 1 - label * count
    base = count * (label - 1)
    bits = jnp.zeros_like(code)
    for a in range(count):
        word = 0
        for b in range(count):
            for turn in range(3):
                word += pattern_ref[a, b] << (30 - turn * count - b)
        bits = jnp.where(block == a, word, bits)
    bits = jnp.where(code == 0, 0, bits)
    both = jnp.transpose(jnp.concatenate([base, bits, jnp.zeros((6, rows), jnp.int32)], axis=0))
    return tuple(jnp.broadcast_to(both[:, i : i + 1], (rows, LANES)) for i in range(2))


def match_rows(left_ref, row_base, row_bits, right_ref, code, same, best):
    rows, columns = left_ref.shape[0], right_ref.shape[0]
    apart = lax.broadcasted_iota(jnp.int32, (rows, LANES), 0) - lax.broadcasted_iota(
        jnp.int32, (rows, LANES), 1
    )
    left = left_ref[...]
    step = 2 * LANES
    for at in range(0, columns, step):
        width = min(step, columns - at)
        sim = dot_nt(left, right_ref[at : at + width, :])
        for piece in range(0, width, LANES):
            span = min(LANES, width - piece)
            begin = at + piece
            gap = code[:, begin : begin + span] - row_base[:, :span]
            gap = jnp.minimum(jnp.maximum(gap, 0), 31)
            fits = jnp.left_shift(row_bits[:, :span], gap) < 0
            if same:
                fits = fits & (apart[:, :span] != begin)
            value = jnp.where(fits, sim[:, piece : piece + span], -1.0)
            if span < LANES:
                value = jnp.concatenate([value, jnp.full((rows, LANES - span), -1.0, F32)], axis=1)
            best = jnp.maximum(best, value)
    return best


def match_own_kernel(chips, own_ref, pattern_ref, best_ref, base_ref, bits_ref):
    code = codes_of(own_ref, chips)
    base, bits = row_words(code, pattern_ref)
    base_ref[...] = base
    bits_ref[...] = bits
    best = jnp.full(base.shape, -1.0, F32)
    best_ref[...] = match_rows(own_ref, base, bits, own_ref, code, True, best)


def by_chip(best, chips):
    across = jnp.max(jnp.transpose(best), axis=0, keepdims=True)
    slots = across.shape[1] // chips
    return [across[:, chip * slots : (chip + 1) * slots] for chip in range(chips)]


def match_other_kernel(
    chips, own_ref, other_ref, before_ref, base_ref, bits_ref, best_ref
):
    slots = own_ref.shape[0] // chips
    code = codes_of(other_ref, chips)
    best = match_rows(
        own_ref, base_ref[...], bits_ref[...], other_ref, code, False, before_ref[...]
    )
    for chip, found in enumerate(by_chip(best, chips)):
        best_ref[chip : chip + 1, 0:slots] = found


def match_more_kernel(
    chips, own_ref, other_ref, more_ref, more_other_ref, base_ref, bits_ref, pattern_ref,
    before_ref, best_ref,
):
    slots, size = own_ref.shape[0] // chips, more_ref.shape[0] // chips
    code, code_other = codes_of(more_ref, chips), codes_of(more_other_ref, chips)
    best = jnp.full((chips * slots, LANES), -1.0, F32)
    base, bits = base_ref[...], bits_ref[...]
    best = match_rows(own_ref, base, bits, more_ref, code, False, best)
    best = match_rows(own_ref, base, bits, more_other_ref, code_other, False, best)
    for chip, found in enumerate(by_chip(best, chips)):
        here = slice(chip, chip + 1)
        best_ref[here, 0:slots] = jnp.maximum(before_ref[here, 0:slots], found)

    base, bits = row_words(code, pattern_ref)
    best = jnp.full((chips * size, LANES), -1.0, F32)
    best = match_rows(more_ref, base, bits, own_ref, codes_of(own_ref, chips), False, best)
    best = match_rows(more_ref, base, bits, other_ref, codes_of(other_ref, chips), False, best)
    best = match_rows(more_ref, base, bits, more_ref, code, True, best)
    best = match_rows(more_ref, base, bits, more_other_ref, code_other, False, best)
    for chip, found in enumerate(by_chip(best, chips)):
        best_ref[chip : chip + 1, slots : slots + size] = found


def unpack_kernel(chips, slots, back_ref, slot_ref, direct_ref, out_ref):
    docs = slot_ref.shape[1]
    back = jnp.transpose(back_ref[...])
    slot_id = lax.broadcasted_iota(jnp.int32, (slots, docs), 0)
    best = jnp.full((slots, docs), -1.0, F32)
    for chip in range(chips):
        here = slot_id == slot_ref[chip : chip + 1, :]
        best = jnp.maximum(best, jnp.where(here, back[0:slots, chip : chip + 1], -1.0))
    out_ref[...] = jnp.maximum(jnp.max(best, axis=0, keepdims=True), direct_ref[...])


def in_vmem():
    return pl.BlockSpec(memory_space=pltpu.VMEM)


def in_smem():
    return pl.BlockSpec(memory_space=pltpu.SMEM)


def params():
    return pltpu.CompilerParams(vmem_limit_bytes=VMEM_LIMIT)


def cost(flops, moved):
    return pl.CostEstimate(flops=flops, bytes_accessed=moved, transcendentals=0)


def send(embeddings, labels, doc_block, assign, count, first, slots):
    groups = lax.axis_size("shard")
    chips = groups * lax.axis_size("grp")
    docs, features = embeddings.shape
    outgoing, slot = pl.pallas_call(
        functools.partial(pack_kernel, groups, chips, first, slots, count),
        out_shape=(
            jax.ShapeDtypeStruct((chips * slots, features), BF16),
            jax.ShapeDtypeStruct((chips, docs), jnp.int32),
        ),
        in_specs=[pl.BlockSpec(memory_space=pl.ANY)] * 4,
        out_specs=(in_vmem(), in_vmem()),
        scratch_shapes=[
            pltpu.VMEM((docs, features), F32),
            pltpu.VMEM((1, docs), jnp.int32),
            pltpu.VMEM((1, docs), jnp.int32),
            pltpu.VMEM((assign.shape[0] // LANES, LANES), jnp.int32),
            pltpu.VMEM((docs, features), BF16),
            pltpu.SemaphoreType.DMA((3 + PIECES,)),
        ],
        compiler_params=params(),
        name="pack",
    )(
        embeddings,
        labels.reshape(1, docs),
        doc_block.reshape(1, docs),
        assign.reshape(-1, LANES),
    )
    arrived = lax.all_to_all(
        outgoing, ("shard", "grp"), split_axis=0, concat_axis=0, tiled=True
    )
    return arrived, slot


def swap(rows):
    cores = lax.axis_size("sub")
    return lax.ppermute(rows, "sub", [(i, (i + 1) % cores) for i in range(cores)])


def per_device(embeddings, labels, doc_block, assign, pattern):
    chips = lax.axis_size("shard") * lax.axis_size("grp")
    docs, features = embeddings.shape
    count = pattern.shape[0]
    mean = docs // chips
    slots = -(-(mean + int(3 * math.sqrt(mean))) // 8) * 8
    rows = chips * slots
    inputs = (embeddings, labels, doc_block, assign)
    work = cost(2 * rows * rows * features, 2 * rows * features)

    own, slot = send(*inputs, count, 0, slots)
    other = swap(own)
    past = own.reshape(chips, slots, features)[:, slots - 1, 2 * LANES : 3 * LANES]
    past = jnp.max(past.astype(F32), axis=0, keepdims=True)
    past = jnp.maximum(past, swap(past))[0, 0].astype(jnp.int32)
    best, base, bits = pl.pallas_call(
        functools.partial(match_own_kernel, chips),
        out_shape=(
            jax.ShapeDtypeStruct((rows, LANES), F32),
            jax.ShapeDtypeStruct((rows, LANES), jnp.int32),
            jax.ShapeDtypeStruct((rows, LANES), jnp.int32),
        ),
        in_specs=[in_vmem(), in_smem()],
        out_specs=(in_vmem(), in_vmem(), in_vmem()),
        compiler_params=params(),
        cost_estimate=work,
        name="match_own",
    )(own, pattern)
    best = pl.pallas_call(
        functools.partial(match_other_kernel, chips),
        out_shape=jax.ShapeDtypeStruct((chips, LANES), F32),
        in_specs=[in_vmem()] * 5,
        out_specs=in_vmem(),
        compiler_params=params(),
        cost_estimate=work,
        name="match_other",
    )(own, other, best, base, bits)

    def second_round(size):
        more, more_slot = send(*inputs, count, slots - 1, size)
        found = pl.pallas_call(
            functools.partial(match_more_kernel, chips),
            out_shape=jax.ShapeDtypeStruct((chips, LANES), F32),
            in_specs=[in_vmem()] * 6 + [in_smem(), in_vmem()],
            out_specs=in_vmem(),
            compiler_params=params(),
            name="match_more",
        )(own, other, more, swap(more), base, bits, pattern, best)
        return found, jnp.where(more_slot >= 0, more_slot + slots, slot), lowest

    def by_general_form():
        direct = general_form(*inputs, pattern).reshape(1, docs)
        return best, jnp.full_like(slot, -1), direct

    lowest = jnp.full((1, docs), -1.0, F32)
    rounds = [lambda: (best, slot, lowest)]
    rounds += [functools.partial(second_round, size) for size in MORE]
    best, slot, direct = lax.switch(past, rounds + [by_general_form])
    back = lax.all_to_all(best, ("shard", "grp"), split_axis=0, concat_axis=0, tiled=True)
    return pl.pallas_call(
        functools.partial(unpack_kernel, chips, slots + max(MORE)),
        out_shape=jax.ShapeDtypeStruct((1, docs), F32),
        in_specs=[in_vmem()] * 3,
        out_specs=in_vmem(),
        compiler_params=params(),
        name="unpack",
    )(back, slot, direct).reshape(docs)


def solution(mesh):
    in_specs = (
        P(("parts", "shard", "grp", "sub"), None),
        P(("parts", "shard", "grp", "sub")),
        P(("parts", "shard", "grp", "sub")),
        P("parts"),
        P(),
    )
    out_specs = P(("parts", "shard", "grp", "sub"))
    return jax.shard_map(
        per_device, mesh=mesh, in_specs=in_specs, out_specs=out_specs, check_vma=False
    )
```

```python
import functools
import math

import jax
import jax.numpy as jnp
from jax import lax
from jax.experimental import pallas as pl
from jax.experimental.pallas import tpu as pltpu
from jax.sharding import PartitionSpec as P

BF16 = jnp.bfloat16
F32 = jnp.float32
VMEM_LIMIT = 32 * 1024 * 1024
LANES = 128
ORDER = [2, 4, 1, 6, 3, 5, 7, 0]
PIECES = 2
MORE = (24, 40)


def row_masks(doc_codes, pattern):
    count = pattern.shape[0]
    powers = jnp.left_shift(jnp.int32(1), jnp.arange(count, dtype=jnp.int32))
    pattern_bits = jnp.sum(pattern * powers[None, :], axis=1)
    block_ids = doc_codes % count
    picked = block_ids[:, None] == jnp.arange(count, dtype=jnp.int32)[None, :]
    return jnp.sum(jnp.where(picked, pattern_bits[None, :], 0), axis=1)


def allowed(row_codes, masks, col_codes, count):
    adjacent = jnp.abs(row_codes[:, None] // count - col_codes[None, :] // count) <= 1
    filled = (col_codes >= 0)[None, :]
    permitted = jnp.right_shift(masks[:, None], col_codes[None, :] % count) % 2 == 1
    return adjacent & filled & permitted


def scores(left_rows, right_rows):
    return lax.dot_general(
        left_rows, right_rows, (((1,), (1,)), ((), ())), preferred_element_type=jnp.float32
    )


def from_members(rows):
    members = lax.axis_size(("grp", "sub"))
    shifts = [[(i, (i + shift) % members) for i in range(members)] for shift in range(1, members)]
    return jnp.concatenate([rows] + [lax.ppermute(rows, ("grp", "sub"), to) for to in shifts])


def general_form(embeddings, labels, doc_block, assign, pattern):
    count = pattern.shape[0]
    group_count = lax.axis_size("shard")
    local_rows = embeddings.shape[0]
    capacity = 2 * local_rows // group_count
    features = embeddings.shape[1]
    unit_rows = (
        embeddings * lax.rsqrt(jnp.sum(embeddings * embeddings, axis=1, keepdims=True) + 1e-06)
    ).astype(jnp.bfloat16)
    target_group = assign[labels]
    one_hot = (target_group[:, None] == jnp.arange(group_count, dtype=jnp.int32)[None, :]).astype(
        jnp.int32
    )
    earlier = jnp.cumsum(one_hot, axis=0) - one_hot
    send_slot = target_group * capacity + jnp.sum(earlier * one_hot, axis=1)
    doc_codes = labels * count + doc_block
    outgoing = (
        jnp.zeros((group_count * capacity, features), jnp.bfloat16).at[send_slot].set(unit_rows)
    )
    outgoing_codes = jnp.full((group_count * capacity,), -1, jnp.int32).at[send_slot].set(doc_codes)
    arrived, arrived_codes = (
        lax.all_to_all(outgoing, "shard", split_axis=0, concat_axis=0, tiled=True),
        lax.all_to_all(outgoing_codes, "shard", split_axis=0, concat_axis=0, tiled=True),
    )
    masks = row_masks(arrived_codes, pattern)
    row_count = arrived.shape[0]
    position = jnp.arange(row_count, dtype=jnp.int32)
    start_value = jnp.full((row_count,), -1.0, jnp.float32)
    columns = from_members(arrived)
    column_codes = from_members(arrived_codes)
    similarity = scores(arrived, columns)
    permitted_pairs = allowed(arrived_codes, masks, column_codes, count)
    column_position = jnp.arange(columns.shape[0], dtype=jnp.int32)
    permitted_pairs = permitted_pairs & (position[:, None] != column_position[None, :])
    best_match = jnp.maximum(
        start_value, jnp.max(jnp.where(permitted_pairs, similarity, -1.0), axis=1)
    )
    returned_max = lax.all_to_all(best_match, "shard", split_axis=0, concat_axis=0, tiled=True)
    return returned_max[send_slot]


def distances(chips):
    return ORDER if chips == 8 else list(range(chips - 1, -1, -1))


def dot_nt(left, right):
    return lax.dot_general(left, right, (((1,), (1,)), ((), ())), preferred_element_type=F32)


def pack_kernel(
    groups, chips, first, slots, count, me_ref, emb_hbm, label_hbm, block_hbm, assign_hbm, *refs
):
    out_refs, slot_ref = refs[:chips], refs[chips]
    emb_ref, label_ref, block_ref, assign_ref, unit_ref, copied = refs[chips + 1 :]
    me = me_ref[0]
    docs, features = emb_hbm.shape
    step = docs // PIECES
    small = [(label_hbm, label_ref), (assign_hbm, assign_ref), (block_hbm, block_ref)]
    moves = list(small)
    for piece in range(PIECES):
        rows = pl.ds(piece * step, step)
        moves.append((emb_hbm.at[rows], emb_ref.at[rows]))
    copies = [
        pltpu.make_async_copy(source, target, copied.at[i])
        for i, (source, target) in enumerate(moves)
    ]
    for copy in copies:
        copy.start()
    for copy in copies[: len(small)]:
        copy.wait()
    labels = label_ref[...]
    clusters = assign_ref.shape[0] * assign_ref.shape[1]
    assign = assign_ref[...]

    group = jnp.zeros((1, docs), jnp.int32)
    start = jnp.zeros((1, docs), jnp.int32)
    stop = jnp.full((1, docs), clusters, jnp.int32)
    for g in range(1, groups):
        bound = jnp.sum((assign < g).astype(F32), axis=0, keepdims=True)
        bound = jnp.sum(bound, axis=1, keepdims=True).astype(jnp.int32)
        inside = labels >= bound
        group = group + inside.astype(jnp.int32)
        start = jnp.where(inside, jnp.maximum(start, bound), start)
        stop = jnp.where(inside, stop, jnp.minimum(stop, bound))
    extent = (stop - start).astype(F32)

    def home_of(cluster):
        above = ((cluster - start + 1) * chips - 1).astype(F32)
        return jnp.floor((above + 0.5) / extent).astype(jnp.int32)

    home = home_of(labels) ^ me
    beside = jnp.where(labels + 1 < stop, home_of(labels + 1) ^ me, home)

    chip_id = lax.broadcasted_iota(jnp.int32, (chips, docs), 0)
    member = (chip_id == home) | (chip_id == beside)
    earlier = (
        lax.broadcasted_iota(jnp.int32, (docs, docs), 0)
        < lax.broadcasted_iota(jnp.int32, (docs, docs), 1)
    ).astype(F32).astype(BF16)
    rank = jnp.dot(
        member.astype(F32).astype(BF16), earlier, preferred_element_type=F32
    ).astype(jnp.int32) - first
    most = jnp.max(jnp.where(member, rank, -1), axis=0, keepdims=True)
    most = jnp.max(most, axis=1, keepdims=True)
    past = jnp.where(most >= slots - 1, 1.0, 0.0)
    for more in MORE:
        past = past + jnp.where(most >= slots + more - 2, 1.0, 0.0)
    slot = jnp.where(member & (rank >= 0) & (rank < slots - 1), rank, -1)
    for chip in range(chips):
        slot_ref[pl.ds(me ^ chip, 1), :] = slot[chip : chip + 1, :]

    code = (labels + group + 2) * count + block_ref[...] + 1
    row_id = lax.broadcasted_iota(jnp.int32, (8, docs), 0)
    digits = jnp.where(row_id == 0, code >> 7, jnp.where(row_id == 1, code & 127, 0))
    digits = digits.astype(F32).astype(BF16)

    slot_id = lax.broadcasted_iota(jnp.int32, (chips, slots, docs), 1)
    picks = (slot_id == slot[:, None, :]).astype(F32).reshape(chips * slots, docs).astype(BF16)

    sent = dot_nt(digits, picks)
    tail = lax.broadcasted_iota(jnp.int32, (8, 3 * LANES), 0) == 7
    fill = jnp.zeros((1, LANES - slots), F32)
    for piece, copy in enumerate(copies[len(small) :]):
        copy.wait()
        rows = slice(piece * step, (piece + 1) * step)
        emb = emb_ref[rows, :]
        scale = lax.rsqrt(jnp.sum(emb * emb, axis=1, keepdims=True) + 1e-06)
        unit_ref[rows, :] = (emb * scale).astype(BF16)
    step = min(features, 4 * LANES)
    for at in range(0, features, step):
        rows = jnp.dot(picks, unit_ref[:, at : at + step], preferred_element_type=F32)
        for chip in range(chips):
            here = rows[chip * slots : (chip + 1) * slots, :]
            out_refs[chip][:, at : at + step] = here.astype(BF16)
    for chip in range(chips):
        here = slice(chip * slots, (chip + 1) * slots)
        row = [sent[0:1, here], fill, sent[1:2, here], fill, jnp.broadcast_to(past, (1, LANES))]
        held = out_refs[chip][slots - 8 : slots, : 3 * LANES].astype(F32)
        held = jnp.where(tail, jnp.concatenate(row, axis=1), held)
        out_refs[chip][slots - 8 : slots, : 3 * LANES] = held.astype(BF16)


def join_kernel(*refs):
    slots = refs[0].shape[0]
    for at, ref in enumerate(refs[:-1]):
        refs[-1][at * slots : (at + 1) * slots, :] = ref[...]


def codes_of(rows_ref, chips):
    slots = rows_ref.shape[0] // chips
    pieces = []
    for end in range(slots, chips * slots + 1, slots):
        sent = rows_ref[end - 8 : end, : 2 * LANES].astype(F32)[7:8, :]
        pieces.append((sent[:, :LANES] * 128.0 + sent[:, LANES:])[:, :slots])
    return jnp.concatenate(pieces, axis=1).astype(jnp.int32)


def row_words(code, pattern_ref):
    rows = code.shape[1]
    count = pattern_ref.shape[0]
    label = jnp.floor((code.astype(F32) - 0.5) / count).astype(jnp.int32)
    block = code - 1 - label * count
    base = count * (label - 1)
    bits = jnp.zeros_like(code)
    for a in range(count):
        word = 0
        for b in range(count):
            for turn in range(3):
                word += pattern_ref[a, b] << (30 - turn * count - b)
        bits = jnp.where(block == a, word, bits)
    bits = jnp.where(code == 0, 0, bits)
    both = jnp.transpose(jnp.concatenate([base, bits, jnp.zeros((6, rows), jnp.int32)], axis=0))
    return tuple(jnp.broadcast_to(both[:, i : i + 1], (rows, LANES)) for i in range(2))


def match_rows(left_ref, row_base, row_bits, right_ref, code, same, best):
    rows, columns = left_ref.shape[0], right_ref.shape[0]
    apart = lax.broadcasted_iota(jnp.int32, (rows, LANES), 0) - lax.broadcasted_iota(
        jnp.int32, (rows, LANES), 1
    )
    left = left_ref[...]
    step = 2 * LANES
    for at in range(0, columns, step):
        width = min(step, columns - at)
        sim = dot_nt(left, right_ref[at : at + width, :])
        for piece in range(0, width, LANES):
            span = min(LANES, width - piece)
            begin = at + piece
            gap = code[:, begin : begin + span] - row_base[:, :span]
            gap = jnp.minimum(jnp.maximum(gap, 0), 31)
            fits = jnp.left_shift(row_bits[:, :span], gap) < 0
            if same:
                fits = fits & (apart[:, :span] != begin)
            value = jnp.where(fits, sim[:, piece : piece + span], -1.0)
            if span < LANES:
                value = jnp.concatenate([value, jnp.full((rows, LANES - span), -1.0, F32)], axis=1)
            best = jnp.maximum(best, value)
    return best


def match_own_kernel(chips, own_ref, pattern_ref, best_ref, base_ref, bits_ref):
    code = codes_of(own_ref, chips)
    base, bits = row_words(code, pattern_ref)
    base_ref[...] = base
    bits_ref[...] = bits
    best = jnp.full(base.shape, -1.0, F32)
    best_ref[...] = match_rows(own_ref, base, bits, own_ref, code, True, best)


def by_chip(best, chips):
    across = jnp.max(jnp.transpose(best), axis=0, keepdims=True)
    slots = across.shape[1] // chips
    return [across[:, chip * slots : (chip + 1) * slots] for chip in range(chips)]


def match_other_kernel(
    chips, me_ref, own_ref, other_ref, before_ref, base_ref, bits_ref, best_ref
):
    slots = own_ref.shape[0] // chips
    code = codes_of(other_ref, chips)
    best = match_rows(
        own_ref, base_ref[...], bits_ref[...], other_ref, code, False, before_ref[...]
    )
    for chip, found in zip(distances(chips), by_chip(best, chips)):
        best_ref[pl.ds(me_ref[0] ^ chip, 1), 0:slots] = found


def match_more_kernel(
    chips, me_ref, own_ref, other_ref, more_ref, more_other_ref, base_ref, bits_ref, pattern_ref,
    before_ref, best_ref,
):
    slots, size = own_ref.shape[0] // chips, more_ref.shape[0] // chips
    code, code_other = codes_of(more_ref, chips), codes_of(more_other_ref, chips)
    best = jnp.full((chips * slots, LANES), -1.0, F32)
    base, bits = base_ref[...], bits_ref[...]
    best = match_rows(own_ref, base, bits, more_ref, code, False, best)
    best = match_rows(own_ref, base, bits, more_other_ref, code_other, False, best)
    for chip, found in zip(distances(chips), by_chip(best, chips)):
        here = pl.ds(me_ref[0] ^ chip, 1)
        best_ref[here, 0:slots] = jnp.maximum(before_ref[here, 0:slots], found)

    base, bits = row_words(code, pattern_ref)
    best = jnp.full((chips * size, LANES), -1.0, F32)
    best = match_rows(more_ref, base, bits, own_ref, codes_of(own_ref, chips), False, best)
    best = match_rows(more_ref, base, bits, other_ref, codes_of(other_ref, chips), False, best)
    best = match_rows(more_ref, base, bits, more_ref, code, True, best)
    best = match_rows(more_ref, base, bits, more_other_ref, code_other, False, best)
    for chip, found in zip(distances(chips), by_chip(best, chips)):
        best_ref[pl.ds(me_ref[0] ^ chip, 1), slots : slots + size] = found


def unpack_kernel(chips, slots, back_ref, slot_ref, direct_ref, out_ref):
    docs = slot_ref.shape[1]
    back = jnp.transpose(back_ref[...])
    slot_id = lax.broadcasted_iota(jnp.int32, (slots, docs), 0)
    best = jnp.full((slots, docs), -1.0, F32)
    for chip in range(chips):
        here = slot_id == slot_ref[chip : chip + 1, :]
        best = jnp.maximum(best, jnp.where(here, back[0:slots, chip : chip + 1], -1.0))
    out_ref[...] = jnp.maximum(jnp.max(best, axis=0, keepdims=True), direct_ref[...])


def in_vmem():
    return pl.BlockSpec(memory_space=pltpu.VMEM)


def in_smem():
    return pl.BlockSpec(memory_space=pltpu.SMEM)


def params():
    return pltpu.CompilerParams(vmem_limit_bytes=VMEM_LIMIT)


def cost(flops, moved):
    return pl.CostEstimate(flops=flops, bytes_accessed=moved, transcendentals=0)


def send(me, embeddings, labels, doc_block, assign, count, first, slots):
    groups = lax.axis_size("shard")
    chips = groups * lax.axis_size("grp")
    docs, features = embeddings.shape
    *outgoing, slot = pl.pallas_call(
        functools.partial(pack_kernel, groups, chips, first, slots, count),
        out_shape=[jax.ShapeDtypeStruct((slots, features), BF16)] * chips
        + [jax.ShapeDtypeStruct((chips, docs), jnp.int32)],
        in_specs=[in_smem()] + [pl.BlockSpec(memory_space=pl.ANY)] * 4,
        out_specs=[in_vmem()] * (chips + 1),
        scratch_shapes=[
            pltpu.VMEM((docs, features), F32),
            pltpu.VMEM((1, docs), jnp.int32),
            pltpu.VMEM((1, docs), jnp.int32),
            pltpu.VMEM((assign.shape[0] // LANES, LANES), jnp.int32),
            pltpu.VMEM((docs, features), BF16),
            pltpu.SemaphoreType.DMA((3 + PIECES,)),
        ],
        compiler_params=params(),
        name="pack",
    )(
        me,
        embeddings,
        labels.reshape(1, docs),
        doc_block.reshape(1, docs),
        assign.reshape(-1, LANES),
    )
    arrived = []
    for away in distances(chips)[:-1]:
        to = [(chip, chip ^ away) for chip in range(chips)]
        arrived.append(lax.ppermute(outgoing[away], ("shard", "grp"), to))
    arrived.append(outgoing[0])
    joined = pl.pallas_call(
        join_kernel,
        out_shape=jax.ShapeDtypeStruct((chips * slots, features), BF16),
        in_specs=[in_vmem()] * chips,
        out_specs=in_vmem(),
        compiler_params=params(),
        name="join",
    )(*arrived)
    return joined, slot


def swap(rows):
    cores = lax.axis_size("sub")
    return lax.ppermute(rows, "sub", [(i, (i + 1) % cores) for i in range(cores)])


def per_device(embeddings, labels, doc_block, assign, pattern):
    chips = lax.axis_size("shard") * lax.axis_size("grp")
    docs, features = embeddings.shape
    count = pattern.shape[0]
    mean = docs // chips
    slots = -(-(mean + int(3 * math.sqrt(mean))) // 8) * 8
    rows = chips * slots
    me = lax.axis_index(("shard", "grp")).astype(jnp.int32).reshape(1)
    inputs = (embeddings, labels, doc_block, assign)
    work = cost(2 * rows * rows * features, 2 * rows * features)

    own, slot = send(me, *inputs, count, 0, slots)
    other = swap(own)
    ends = [
        rows_in.reshape(chips, slots, features)[:, slots - 1, 2 * LANES : 3 * LANES]
        for rows_in in (own, other)
    ]
    past = jnp.maximum(*[jnp.max(end.astype(F32), axis=0, keepdims=True) for end in ends])
    past = past[0, 0].astype(jnp.int32)
    best, base, bits = pl.pallas_call(
        functools.partial(match_own_kernel, chips),
        out_shape=(
            jax.ShapeDtypeStruct((rows, LANES), F32),
            jax.ShapeDtypeStruct((rows, LANES), jnp.int32),
            jax.ShapeDtypeStruct((rows, LANES), jnp.int32),
        ),
        in_specs=[in_vmem(), in_smem()],
        out_specs=(in_vmem(), in_vmem(), in_vmem()),
        compiler_params=params(),
        cost_estimate=work,
        name="match_own",
    )(own, pattern)
    best = pl.pallas_call(
        functools.partial(match_other_kernel, chips),
        out_shape=jax.ShapeDtypeStruct((chips, LANES), F32),
        in_specs=[in_smem()] + [in_vmem()] * 5,
        out_specs=in_vmem(),
        compiler_params=params(),
        cost_estimate=work,
        name="match_other",
    )(me, own, other, best, base, bits)

    def second_round(size):
        more, more_slot = send(me, *inputs, count, slots - 1, size)
        found = pl.pallas_call(
            functools.partial(match_more_kernel, chips),
            out_shape=jax.ShapeDtypeStruct((chips, LANES), F32),
            in_specs=[in_smem()] + [in_vmem()] * 6 + [in_smem(), in_vmem()],
            out_specs=in_vmem(),
            compiler_params=params(),
            name="match_more",
        )(me, own, other, more, swap(more), base, bits, pattern, best)
        return found, jnp.where(more_slot >= 0, more_slot + slots, slot), lowest

    def by_general_form():
        direct = general_form(*inputs, pattern).reshape(1, docs)
        return best, jnp.full_like(slot, -1), direct

    lowest = jnp.full((1, docs), -1.0, F32)
    rounds = [lambda: (best, slot, lowest)]
    rounds += [functools.partial(second_round, size) for size in MORE]
    best, slot, direct = lax.switch(past, rounds + [by_general_form])
    back = lax.all_to_all(best, ("shard", "grp"), split_axis=0, concat_axis=0, tiled=True)
    return pl.pallas_call(
        functools.partial(unpack_kernel, chips, slots + max(MORE)),
        out_shape=jax.ShapeDtypeStruct((1, docs), F32),
        in_specs=[in_vmem()] * 3,
        out_specs=in_vmem(),
        compiler_params=params(),
        name="unpack",
    )(back, slot, direct).reshape(docs)


def solution(mesh):
    in_specs = (
        P(("parts", "shard", "grp", "sub"), None),
        P(("parts", "shard", "grp", "sub")),
        P(("parts", "shard", "grp", "sub")),
        P("parts"),
        P(),
    )
    out_specs = P(("parts", "shard", "grp", "sub"))
    return jax.shard_map(
        per_device, mesh=mesh, in_specs=in_specs, out_specs=out_specs, check_vma=False
    )
```

```python
import functools
import math

import jax
import jax.numpy as jnp
from jax import lax
from jax.experimental import pallas as pl
from jax.experimental.pallas import tpu as pltpu
from jax.sharding import PartitionSpec as P

BF16 = jnp.bfloat16
F32 = jnp.float32
VMEM_LIMIT = 32 * 1024 * 1024
LANES = 128
ORDER = [2, 4, 1, 6, 3, 5, 7, 0]
PIECES = 2
MORE = (8, 24, 40)


def row_masks(doc_codes, pattern):
    count = pattern.shape[0]
    powers = jnp.left_shift(jnp.int32(1), jnp.arange(count, dtype=jnp.int32))
    pattern_bits = jnp.sum(pattern * powers[None, :], axis=1)
    block_ids = doc_codes % count
    picked = block_ids[:, None] == jnp.arange(count, dtype=jnp.int32)[None, :]
    return jnp.sum(jnp.where(picked, pattern_bits[None, :], 0), axis=1)


def allowed(row_codes, masks, col_codes, count):
    adjacent = jnp.abs(row_codes[:, None] // count - col_codes[None, :] // count) <= 1
    filled = (col_codes >= 0)[None, :]
    permitted = jnp.right_shift(masks[:, None], col_codes[None, :] % count) % 2 == 1
    return adjacent & filled & permitted


def scores(left_rows, right_rows):
    return lax.dot_general(
        left_rows, right_rows, (((1,), (1,)), ((), ())), preferred_element_type=jnp.float32
    )


def from_members(rows):
    members = lax.axis_size(("grp", "sub"))
    shifts = [[(i, (i + shift) % members) for i in range(members)] for shift in range(1, members)]
    return jnp.concatenate([rows] + [lax.ppermute(rows, ("grp", "sub"), to) for to in shifts])


def general_form(embeddings, labels, doc_block, assign, pattern):
    count = pattern.shape[0]
    group_count = lax.axis_size("shard")
    local_rows = embeddings.shape[0]
    capacity = 2 * local_rows // group_count
    features = embeddings.shape[1]
    unit_rows = (
        embeddings * lax.rsqrt(jnp.sum(embeddings * embeddings, axis=1, keepdims=True) + 1e-06)
    ).astype(jnp.bfloat16)
    target_group = assign[labels]
    one_hot = (target_group[:, None] == jnp.arange(group_count, dtype=jnp.int32)[None, :]).astype(
        jnp.int32
    )
    earlier = jnp.cumsum(one_hot, axis=0) - one_hot
    send_slot = target_group * capacity + jnp.sum(earlier * one_hot, axis=1)
    doc_codes = labels * count + doc_block
    outgoing = (
        jnp.zeros((group_count * capacity, features), jnp.bfloat16).at[send_slot].set(unit_rows)
    )
    outgoing_codes = jnp.full((group_count * capacity,), -1, jnp.int32).at[send_slot].set(doc_codes)
    arrived, arrived_codes = (
        lax.all_to_all(outgoing, "shard", split_axis=0, concat_axis=0, tiled=True),
        lax.all_to_all(outgoing_codes, "shard", split_axis=0, concat_axis=0, tiled=True),
    )
    masks = row_masks(arrived_codes, pattern)
    row_count = arrived.shape[0]
    position = jnp.arange(row_count, dtype=jnp.int32)
    start_value = jnp.full((row_count,), -1.0, jnp.float32)
    columns = from_members(arrived)
    column_codes = from_members(arrived_codes)
    similarity = scores(arrived, columns)
    permitted_pairs = allowed(arrived_codes, masks, column_codes, count)
    column_position = jnp.arange(columns.shape[0], dtype=jnp.int32)
    permitted_pairs = permitted_pairs & (position[:, None] != column_position[None, :])
    best_match = jnp.maximum(
        start_value, jnp.max(jnp.where(permitted_pairs, similarity, -1.0), axis=1)
    )
    returned_max = lax.all_to_all(best_match, "shard", split_axis=0, concat_axis=0, tiled=True)
    return returned_max[send_slot]


def distances(chips):
    return ORDER if chips == 8 else list(range(chips - 1, -1, -1))


def dot_nt(left, right):
    return lax.dot_general(left, right, (((1,), (1,)), ((), ())), preferred_element_type=F32)


def pack_kernel(
    groups, chips, first, slots, count, me_ref, emb_hbm, label_hbm, block_hbm, assign_hbm, *refs
):
    out_refs, slot_ref = refs[:chips], refs[chips]
    emb_ref, label_ref, block_ref, assign_ref, unit_ref, copied = refs[chips + 1 :]
    me = me_ref[0]
    docs, features = emb_hbm.shape
    step = docs // PIECES
    small = [(label_hbm, label_ref), (assign_hbm, assign_ref), (block_hbm, block_ref)]
    moves = list(small)
    for piece in range(PIECES):
        rows = pl.ds(piece * step, step)
        moves.append((emb_hbm.at[rows], emb_ref.at[rows]))
    copies = [
        pltpu.make_async_copy(source, target, copied.at[i])
        for i, (source, target) in enumerate(moves)
    ]
    for copy in copies:
        copy.start()
    for copy in copies[: len(small)]:
        copy.wait()
    labels = label_ref[...]
    clusters = assign_ref.shape[0] * assign_ref.shape[1]
    assign = assign_ref[...]

    group = jnp.zeros((1, docs), jnp.int32)
    start = jnp.zeros((1, docs), jnp.int32)
    stop = jnp.full((1, docs), clusters, jnp.int32)
    for g in range(1, groups):
        bound = jnp.sum((assign < g).astype(F32), axis=0, keepdims=True)
        bound = jnp.sum(bound, axis=1, keepdims=True).astype(jnp.int32)
        inside = labels >= bound
        group = group + inside.astype(jnp.int32)
        start = jnp.where(inside, jnp.maximum(start, bound), start)
        stop = jnp.where(inside, stop, jnp.minimum(stop, bound))
    extent = (stop - start).astype(F32)

    def home_of(cluster):
        above = ((cluster - start + 1) * chips - 1).astype(F32)
        return jnp.floor((above + 0.5) / extent).astype(jnp.int32)

    home = home_of(labels) ^ me
    beside = jnp.where(labels + 1 < stop, home_of(labels + 1) ^ me, home)

    chip_id = lax.broadcasted_iota(jnp.int32, (chips, docs), 0)
    member = (chip_id == home) | (chip_id == beside)
    earlier = (
        lax.broadcasted_iota(jnp.int32, (docs, docs), 0)
        < lax.broadcasted_iota(jnp.int32, (docs, docs), 1)
    ).astype(F32).astype(BF16)
    rank = jnp.dot(
        member.astype(F32).astype(BF16), earlier, preferred_element_type=F32
    ).astype(jnp.int32) - first
    most = jnp.max(jnp.where(member, rank, -1), axis=0, keepdims=True)
    most = jnp.max(most, axis=1, keepdims=True)
    past = jnp.where(most >= slots - 1, 1.0, 0.0)
    for more in MORE:
        past = past + jnp.where(most >= slots + more - 2, 1.0, 0.0)
    slot = jnp.where(member & (rank >= 0) & (rank < slots - 1), rank, -1)
    for chip in range(chips):
        slot_ref[pl.ds(me ^ chip, 1), :] = slot[chip : chip + 1, :]

    code = (labels + group + 2) * count + block_ref[...] + 1
    row_id = lax.broadcasted_iota(jnp.int32, (8, docs), 0)
    digits = jnp.where(row_id == 0, code >> 7, jnp.where(row_id == 1, code & 127, 0))
    digits = digits.astype(F32).astype(BF16)

    slot_id = lax.broadcasted_iota(jnp.int32, (chips, slots, docs), 1)
    picks = (slot_id == slot[:, None, :]).astype(F32).reshape(chips * slots, docs).astype(BF16)

    sent = dot_nt(digits, picks)
    tail = lax.broadcasted_iota(jnp.int32, (8, 3 * LANES), 0) == 7
    fill = jnp.zeros((1, LANES - slots), F32)
    for piece, copy in enumerate(copies[len(small) :]):
        copy.wait()
        rows = slice(piece * step, (piece + 1) * step)
        emb = emb_ref[rows, :]
        scale = lax.rsqrt(jnp.sum(emb * emb, axis=1, keepdims=True) + 1e-06)
        unit_ref[rows, :] = (emb * scale).astype(BF16)
    step = min(features, 4 * LANES)
    for at in range(0, features, step):
        rows = jnp.dot(picks, unit_ref[:, at : at + step], preferred_element_type=F32)
        for chip in range(chips):
            here = rows[chip * slots : (chip + 1) * slots, :]
            out_refs[chip][:, at : at + step] = here.astype(BF16)
    for chip in range(chips):
        here = slice(chip * slots, (chip + 1) * slots)
        row = [sent[0:1, here], fill, sent[1:2, here], fill, jnp.broadcast_to(past, (1, LANES))]
        held = out_refs[chip][slots - 8 : slots, : 3 * LANES].astype(F32)
        held = jnp.where(tail, jnp.concatenate(row, axis=1), held)
        out_refs[chip][slots - 8 : slots, : 3 * LANES] = held.astype(BF16)


def join_kernel(*refs):
    slots = refs[0].shape[0]
    for at, ref in enumerate(refs[:-1]):
        refs[-1][at * slots : (at + 1) * slots, :] = ref[...]


def codes_of(rows_ref, chips):
    slots = rows_ref.shape[0] // chips
    pieces = []
    for end in range(slots, chips * slots + 1, slots):
        sent = rows_ref[end - 8 : end, : 2 * LANES].astype(F32)[7:8, :]
        pieces.append((sent[:, :LANES] * 128.0 + sent[:, LANES:])[:, :slots])
    return jnp.concatenate(pieces, axis=1).astype(jnp.int32)


def row_words(code, pattern_ref):
    rows = code.shape[1]
    count = pattern_ref.shape[0]
    label = jnp.floor((code.astype(F32) - 0.5) / count).astype(jnp.int32)
    block = code - 1 - label * count
    base = count * (label - 1)
    bits = jnp.zeros_like(code)
    for a in range(count):
        word = 0
        for b in range(count):
            for turn in range(3):
                word += pattern_ref[a, b] << (30 - turn * count - b)
        bits = jnp.where(block == a, word, bits)
    bits = jnp.where(code == 0, 0, bits)
    both = jnp.transpose(jnp.concatenate([base, bits, jnp.zeros((6, rows), jnp.int32)], axis=0))
    return tuple(jnp.broadcast_to(both[:, i : i + 1], (rows, LANES)) for i in range(2))


def match_rows(left_ref, row_base, row_bits, right_ref, code, same, best):
    rows, columns = left_ref.shape[0], right_ref.shape[0]
    apart = lax.broadcasted_iota(jnp.int32, (rows, LANES), 0) - lax.broadcasted_iota(
        jnp.int32, (rows, LANES), 1
    )
    left = left_ref[...]
    step = 2 * LANES
    for at in range(0, columns, step):
        width = min(step, columns - at)
        sim = dot_nt(left, right_ref[at : at + width, :])
        for piece in range(0, width, LANES):
            span = min(LANES, width - piece)
            begin = at + piece
            gap = code[:, begin : begin + span] - row_base[:, :span]
            gap = jnp.minimum(jnp.maximum(gap, 0), 31)
            fits = jnp.left_shift(row_bits[:, :span], gap) < 0
            if same:
                fits = fits & (apart[:, :span] != begin)
            value = jnp.where(fits, sim[:, piece : piece + span], -1.0)
            if span < LANES:
                value = jnp.concatenate([value, jnp.full((rows, LANES - span), -1.0, F32)], axis=1)
            best = jnp.maximum(best, value)
    return best


def match_own_kernel(chips, own_ref, pattern_ref, best_ref, base_ref, bits_ref):
    code = codes_of(own_ref, chips)
    base, bits = row_words(code, pattern_ref)
    base_ref[...] = base
    bits_ref[...] = bits
    best = jnp.full(base.shape, -1.0, F32)
    best_ref[...] = match_rows(own_ref, base, bits, own_ref, code, True, best)


def by_chip(best, chips):
    across = jnp.max(jnp.transpose(best), axis=0, keepdims=True)
    slots = across.shape[1] // chips
    return [across[:, chip * slots : (chip + 1) * slots] for chip in range(chips)]


def match_other_kernel(
    chips, me_ref, own_ref, other_ref, before_ref, base_ref, bits_ref, best_ref
):
    slots = own_ref.shape[0] // chips
    code = codes_of(other_ref, chips)
    best = match_rows(
        own_ref, base_ref[...], bits_ref[...], other_ref, code, False, before_ref[...]
    )
    for chip, found in zip(distances(chips), by_chip(best, chips)):
        best_ref[pl.ds(me_ref[0] ^ chip, 1), 0:slots] = found


def match_more_kernel(
    chips, me_ref, own_ref, other_ref, more_ref, more_other_ref, base_ref, bits_ref, pattern_ref,
    before_ref, best_ref,
):
    slots, size = own_ref.shape[0] // chips, more_ref.shape[0] // chips
    code, code_other = codes_of(more_ref, chips), codes_of(more_other_ref, chips)
    best = jnp.full((chips * slots, LANES), -1.0, F32)
    base, bits = base_ref[...], bits_ref[...]
    best = match_rows(own_ref, base, bits, more_ref, code, False, best)
    best = match_rows(own_ref, base, bits, more_other_ref, code_other, False, best)
    for chip, found in zip(distances(chips), by_chip(best, chips)):
        here = pl.ds(me_ref[0] ^ chip, 1)
        best_ref[here, 0:slots] = jnp.maximum(before_ref[here, 0:slots], found)

    base, bits = row_words(code, pattern_ref)
    best = jnp.full((chips * size, LANES), -1.0, F32)
    best = match_rows(more_ref, base, bits, own_ref, codes_of(own_ref, chips), False, best)
    best = match_rows(more_ref, base, bits, other_ref, codes_of(other_ref, chips), False, best)
    best = match_rows(more_ref, base, bits, more_ref, code, True, best)
    best = match_rows(more_ref, base, bits, more_other_ref, code_other, False, best)
    for chip, found in zip(distances(chips), by_chip(best, chips)):
        best_ref[pl.ds(me_ref[0] ^ chip, 1), slots : slots + size] = found


def unpack_kernel(chips, slots, back_ref, slot_ref, direct_ref, out_ref):
    docs = slot_ref.shape[1]
    back = jnp.transpose(back_ref[...])
    slot_id = lax.broadcasted_iota(jnp.int32, (slots, docs), 0)
    best = jnp.full((slots, docs), -1.0, F32)
    for chip in range(chips):
        here = slot_id == slot_ref[chip : chip + 1, :]
        best = jnp.maximum(best, jnp.where(here, back[0:slots, chip : chip + 1], -1.0))
    out_ref[...] = jnp.maximum(jnp.max(best, axis=0, keepdims=True), direct_ref[...])


def in_vmem():
    return pl.BlockSpec(memory_space=pltpu.VMEM)


def in_smem():
    return pl.BlockSpec(memory_space=pltpu.SMEM)


def params():
    return pltpu.CompilerParams(vmem_limit_bytes=VMEM_LIMIT)


def cost(flops, moved):
    return pl.CostEstimate(flops=flops, bytes_accessed=moved, transcendentals=0)


def send(me, embeddings, labels, doc_block, assign, count, first, slots):
    groups = lax.axis_size("shard")
    chips = groups * lax.axis_size("grp")
    docs, features = embeddings.shape
    *outgoing, slot = pl.pallas_call(
        functools.partial(pack_kernel, groups, chips, first, slots, count),
        out_shape=[jax.ShapeDtypeStruct((slots, features), BF16)] * chips
        + [jax.ShapeDtypeStruct((chips, docs), jnp.int32)],
        in_specs=[in_smem()] + [pl.BlockSpec(memory_space=pl.ANY)] * 4,
        out_specs=[in_vmem()] * (chips + 1),
        scratch_shapes=[
            pltpu.VMEM((docs, features), F32),
            pltpu.VMEM((1, docs), jnp.int32),
            pltpu.VMEM((1, docs), jnp.int32),
            pltpu.VMEM((assign.shape[0] // LANES, LANES), jnp.int32),
            pltpu.VMEM((docs, features), BF16),
            pltpu.SemaphoreType.DMA((3 + PIECES,)),
        ],
        compiler_params=params(),
        name="pack",
    )(
        me,
        embeddings,
        labels.reshape(1, docs),
        doc_block.reshape(1, docs),
        assign.reshape(-1, LANES),
    )
    arrived = []
    for away in distances(chips)[:-1]:
        to = [(chip, chip ^ away) for chip in range(chips)]
        arrived.append(lax.ppermute(outgoing[away], ("shard", "grp"), to))
    arrived.append(outgoing[0])
    joined = pl.pallas_call(
        join_kernel,
        out_shape=jax.ShapeDtypeStruct((chips * slots, features), BF16),
        in_specs=[in_vmem()] * chips,
        out_specs=in_vmem(),
        compiler_params=params(),
        name="join",
    )(*arrived)
    return joined, slot


def swap(rows):
    cores = lax.axis_size("sub")
    return lax.ppermute(rows, "sub", [(i, (i + 1) % cores) for i in range(cores)])


def per_device(embeddings, labels, doc_block, assign, pattern):
    chips = lax.axis_size("shard") * lax.axis_size("grp")
    docs, features = embeddings.shape
    count = pattern.shape[0]
    mean = docs // chips
    slots = -(-(mean + int(3 * math.sqrt(mean))) // 8) * 8
    rows = chips * slots
    me = lax.axis_index(("shard", "grp")).astype(jnp.int32).reshape(1)
    inputs = (embeddings, labels, doc_block, assign)
    work = cost(2 * rows * rows * features, 2 * rows * features)

    own, slot = send(me, *inputs, count, 0, slots)
    other = swap(own)
    ends = [
        rows_in.reshape(chips, slots, features)[:, slots - 1, 2 * LANES : 3 * LANES]
        for rows_in in (own, other)
    ]
    past = jnp.maximum(*[jnp.max(end.astype(F32), axis=0, keepdims=True) for end in ends])
    past = past[0, 0].astype(jnp.int32)
    best, base, bits = pl.pallas_call(
        functools.partial(match_own_kernel, chips),
        out_shape=(
            jax.ShapeDtypeStruct((rows, LANES), F32),
            jax.ShapeDtypeStruct((rows, LANES), jnp.int32),
            jax.ShapeDtypeStruct((rows, LANES), jnp.int32),
        ),
        in_specs=[in_vmem(), in_smem()],
        out_specs=(in_vmem(), in_vmem(), in_vmem()),
        compiler_params=params(),
        cost_estimate=work,
        name="match_own",
    )(own, pattern)
    best = pl.pallas_call(
        functools.partial(match_other_kernel, chips),
        out_shape=jax.ShapeDtypeStruct((chips, LANES), F32),
        in_specs=[in_smem()] + [in_vmem()] * 5,
        out_specs=in_vmem(),
        compiler_params=params(),
        cost_estimate=work,
        name="match_other",
    )(me, own, other, best, base, bits)

    def second_round(size):
        more, more_slot = send(me, *inputs, count, slots - 1, size)
        found = pl.pallas_call(
            functools.partial(match_more_kernel, chips),
            out_shape=jax.ShapeDtypeStruct((chips, LANES), F32),
            in_specs=[in_smem()] + [in_vmem()] * 6 + [in_smem(), in_vmem()],
            out_specs=in_vmem(),
            compiler_params=params(),
            name="match_more",
        )(me, own, other, more, swap(more), base, bits, pattern, best)
        return found, jnp.where(more_slot >= 0, more_slot + slots, slot), lowest

    def by_general_form():
        direct = general_form(*inputs, pattern).reshape(1, docs)
        return best, jnp.full_like(slot, -1), direct

    lowest = jnp.full((1, docs), -1.0, F32)
    rounds = [lambda: (best, slot, lowest)]
    rounds += [functools.partial(second_round, size) for size in MORE]
    best, slot, direct = lax.switch(past, rounds + [by_general_form])
    back = lax.all_to_all(best, ("shard", "grp"), split_axis=0, concat_axis=0, tiled=True)
    return pl.pallas_call(
        functools.partial(unpack_kernel, chips, slots + max(MORE)),
        out_shape=jax.ShapeDtypeStruct((1, docs), F32),
        in_specs=[in_vmem()] * 3,
        out_specs=in_vmem(),
        compiler_params=params(),
        name="unpack",
    )(back, slot, direct).reshape(docs)


def solution(mesh):
    in_specs = (
        P(("parts", "shard", "grp", "sub"), None),
        P(("parts", "shard", "grp", "sub")),
        P(("parts", "shard", "grp", "sub")),
        P("parts"),
        P(),
    )
    out_specs = P(("parts", "shard", "grp", "sub"))
    return jax.shard_map(
        per_device, mesh=mesh, in_specs=in_specs, out_specs=out_specs, check_vma=False
    )
```
